32 devices in a mesh: mem: 8 (over y, x, core), head: 4 (over z).
Axes of the slice: x: 2, y: 2, z: 4, core: 2. Of those that a mesh axis runs over, the one named last changes fastest.
Arguments:
- queries: bfloat16 [4096, 6144], P(('mem', 'head')), may hold values from -18 to 18
- keys_local: bfloat16 [4096, 6144], P(('mem', 'head')), may hold values from -15 to 15
- values_local: bfloat16 [4096, 6144], P(('mem', 'head')), may hold values from -6 to 6
- cache_keys: bfloat16 [4096, 6144], P('mem', 'head'), may hold values from -6 to 6
- cache_values: bfloat16 [4096, 6144], P('mem', 'head'), may hold values from -6 to 6
- block_map: int32 [64], replicated, may hold values from 0 to 63, as said below
- retrieved: int32 [64, 16, 4], P('mem', 'head'), may hold values from 0 to 63, as said below
- out_grad: bfloat16 [4096, 6144], P(('mem', 'head')), may hold values from -24 to 24
Outputs:
- grad_queries: bfloat16 [4096, 6144], P(('mem', 'head'))
- grad_keys_local: bfloat16 [4096, 6144], P(('mem', 'head'))
- grad_values_local: bfloat16 [4096, 6144], P(('mem', 'head'))
- grad_cache_keys: bfloat16 [4096, 6144], P('mem', 'head')
- grad_cache_values: bfloat16 [4096, 6144], P('mem', 'head')
The draws below stay inside these ranges and needn't reach their ends.
Inputs may be any that keep to these rules, and one draw needn't show every extreme that they name: block_map is a permutation of the block ids; block b is stored as block block_map[b] % 8 of index block_map[b] // 8 of mem. `retrieved`: for each head group and each aligned run of 8 query blocks, the 32 ids are distinct and at most 5 of them are stored on one index of mem; in every draw some index of mem stores exactly 5 of them for every run and every group.
All inputs are finite; a program needn't handle non-finite values.
Results may differ from the reference program's by a relative error of at most 0.012.
The reference program's roundings to bfloat16 on the way count: a program that leaves them out, or rounds other values in their place, can miss the bound.
Values may be sent and summed in bfloat16 or wider, within the bound.
No kernel may reach another device: no remote copies, remote signals or barrier semaphores. Data moves between devices by JAX's collectives and lax.ppermute only.
A program may use at most 256 MiB of HBM per device.

```python
import math
import jax
import jax.numpy as jnp
from jax import lax

HEADS = 48
HEAD_DIM = 128
GROUP_HEADS = 3
BLOCK = 64
READS = 4
WINDOW = 512
HEAD_GROUP_COUNT = 16
QB_DEV = 8
BLK_DEV = 8
TOKENS = 4096
QBLOCKS = 64
MEMTOK = 4096
MEMBLOCKS = 64
LENGTH = 4096
CAP = 5


def storage_tables(key):
    perm_key = jax.random.fold_in(key, 3)
    placed = jax.random.permutation(perm_key, MEMBLOCKS).astype(jnp.int32)
    inverse = jnp.argsort(placed, stable=True).astype(jnp.int32)
    return (placed, inverse)


def draw_block_map(key, part):
    return storage_tables(key)[0]


def draw_retrieved(key, part):
    placed, inverse = storage_tables(key)
    device_list = QBLOCKS // QB_DEV
    every_owner = MEMBLOCKS // BLK_DEV
    req_count = QB_DEV * READS
    memory_slot_count = every_owner * CAP
    base_key = jax.random.fold_in(key, 5)
    key_hot, key_heat, key_score, key_start, key_order = jax.random.split(base_key, 5)
    hottest_blocks = jax.random.randint(key_hot, (), 0, every_owner)
    access_heat = jax.random.randint(key_heat, (every_owner,), 0, 4)
    owner_preference = access_heat * 4096 + jnp.where(jnp.arange(every_owner) == hottest_blocks, 1 << 20, 0)
    score_jitter = jax.random.randint(key_score, (device_list, HEAD_GROUP_COUNT, every_owner, CAP), 0, 4096)
    ranked_blocks = (score_jitter + owner_preference[None, None, :, None]).reshape(device_list, HEAD_GROUP_COUNT, memory_slot_count) * memory_slot_count + jnp.arange(memory_slot_count)
    chosen = lax.top_k(ranked_blocks, req_count)[1]
    owner_ids = chosen // CAP
    copy_rank = chosen % CAP
    starts = jax.random.randint(key_start, (device_list, HEAD_GROUP_COUNT, every_owner), 0, BLK_DEV)
    first_local = jnp.take_along_axis(starts, owner_ids, axis=-1)
    stored = owner_ids * BLK_DEV + (first_local + copy_rank) % BLK_DEV
    block_ids = inverse[stored]
    shuffle = jax.random.randint(key_order, (device_list, HEAD_GROUP_COUNT, req_count), 0, 1 << 16) * req_count + jnp.arange(req_count)
    order_idx = jnp.argsort(shuffle, axis=-1, stable=True)
    block_ids = jnp.take_along_axis(block_ids, order_idx, axis=-1)
    block_ids = jnp.transpose(block_ids.reshape(device_list, HEAD_GROUP_COUNT, QB_DEV, READS), (0, 2, 1, 3))
    return block_ids.reshape(QBLOCKS, HEAD_GROUP_COUNT, READS).astype(jnp.int32)


def drawn_pair(key):
    pair_key = jax.random.fold_in(key, 11)
    keys_split = jax.random.split(pair_key, 2)
    features = HEADS * HEAD_DIM
    query_base = jnp.clip(jax.random.normal(keys_split[0], (TOKENS, features), jnp.float32), -4.0, 4.0)
    key_base = jnp.clip(jax.random.normal(keys_split[1], (TOKENS, features), jnp.float32), -4.0, 4.0)
    query_rows = query_base
    key_rows = key_base
    return (query_rows, key_rows)


def draw_queries(key, part):
    return drawn_pair(key)[0].astype(jnp.bfloat16)


def draw_keys_local(key, part):
    return drawn_pair(key)[1].astype(jnp.bfloat16)


def shard_levels(key, shape, shards, low, largest):
    loudness, own = 1.0, jax.random.fold_in(key, 6)
    for axis_at, blocks in shards:
        steps = jnp.exp(jax.random.uniform(jax.random.fold_in(own, axis_at), (blocks,), jnp.float32, low / len(shards), largest / len(shards)))
        loudness = loudness * jnp.repeat(steps, shape[axis_at] // blocks).reshape([-1 if axis == axis_at else 1 for axis in range(len(shape))])
    return loudness


def centred(own_key, extent, spread, limit, shards=(), kind=jnp.bfloat16):
    loudness = shard_levels(own_key, extent, shards, -0.22, 0.18) if shards else 1.0
    values = jax.random.normal(own_key, extent, jnp.float32) * spread * loudness
    return jnp.minimum(jnp.maximum(values, -limit), limit).astype(kind)


def setup_inputs(seed: int = 0) -> dict:
    keys = jax.random.split(jax.random.key(seed), 9)
    return {
        "queries": draw_queries(jax.random.fold_in(keys[8], 71), 0),
        "keys_local": draw_keys_local(jax.random.fold_in(keys[8], 71), 0),
        "values_local": centred(keys[2], (TOKENS, HEADS * HEAD_DIM), 1.0, 6.0, ((0, 32),)),
        "cache_keys": centred(keys[3], (MEMTOK, HEADS * HEAD_DIM), 1.0, 6.0, ((0, 8), (1, 4))),
        "cache_values": centred(keys[4], (MEMTOK, HEADS * HEAD_DIM), 1.0, 6.0, ((0, 8), (1, 4))),
        "block_map": draw_block_map(jax.random.fold_in(keys[8], 71), 0),
        "retrieved": draw_retrieved(jax.random.fold_in(keys[8], 71), 0),
        "out_grad": centred(keys[7], (TOKENS, HEADS * HEAD_DIM), 4.0, 24.0, ((0, 32),)),
    }


def rounded(values):
    return lax.optimization_barrier(values.astype(jnp.bfloat16)).astype(jnp.float32)

def reference(queries, keys_local, values_local, cache_keys, cache_values, block_map, retrieved, out_grad):
    group_width = GROUP_HEADS * HEAD_DIM
    win_blocks = WINDOW // BLOCK
    win_span = (win_blocks + 1) * BLOCK
    mem_span = READS * BLOCK
    scaling = 1.0 / math.sqrt(HEAD_DIM)
    storage = jnp.take(block_map, retrieved, axis=0).astype(jnp.int32)
    query_off = jnp.arange(BLOCK, dtype=jnp.int32)
    key_off = jnp.arange(win_span, dtype=jnp.int32)
    head_shape = (BLOCK, GROUP_HEADS, HEAD_DIM)

    def one_group(group):
        start_col = group * group_width

        def columns(array):
            return lax.dynamic_slice_in_dim(array, start_col, group_width, 1)
        query_g = columns(queries)
        grad_g = columns(out_grad)
        padding = jnp.zeros((WINDOW, group_width), keys_local.dtype)
        key_ext = jnp.concatenate([padding, columns(keys_local)], 0)
        value_ext = jnp.concatenate([padding, columns(values_local)], 0)
        cache_k = columns(cache_keys).reshape(MEMBLOCKS, BLOCK, group_width)
        cache_v = columns(cache_values).reshape(MEMBLOCKS, BLOCK, group_width)
        reads = lax.dynamic_index_in_dim(storage, group, 1, keepdims=False)

        def step(carry, block):
            acc_k, acc_v, mem_k, mem_v = carry
            first = block * BLOCK
            query_b = lax.dynamic_slice_in_dim(query_g, first, BLOCK, 0).astype(jnp.float32).reshape(head_shape)
            grad_b = lax.dynamic_slice_in_dim(grad_g, first, BLOCK, 0).astype(jnp.float32).reshape(head_shape)
            local_k = lax.dynamic_slice_in_dim(key_ext, first, win_span, 0).astype(jnp.float32).reshape(win_span, GROUP_HEADS, HEAD_DIM)
            local_v = lax.dynamic_slice_in_dim(value_ext, first, win_span, 0).astype(jnp.float32).reshape(win_span, GROUP_HEADS, HEAD_DIM)
            which = reads[block]
            read_k = cache_k[which].astype(jnp.float32).reshape(mem_span, GROUP_HEADS, HEAD_DIM)
            read_v = cache_v[which].astype(jnp.float32).reshape(mem_span, GROUP_HEADS, HEAD_DIM)
            tok_q = first + query_off
            tok_k = first - WINDOW + key_off
            allowed = (tok_k[None, :] <= tok_q[:, None]) & (tok_k[None, :] >= tok_q[:, None] - WINDOW) & (tok_k[None, :] >= (tok_q // LENGTH * LENGTH)[:, None])
            score_loc = jnp.einsum('ihd,jhd->hij', query_b, local_k) * scaling
            score_loc = jnp.where(allowed[None], score_loc, -jnp.inf)
            score_mem = jnp.einsum('ihd,jhd->hij', query_b, read_k) * scaling
            row_max = jnp.maximum(lax.optimization_barrier(jnp.max(score_loc, -1)), lax.optimization_barrier(jnp.max(score_mem, -1)))[..., None]
            exp_loc = jnp.exp(score_loc - row_max)
            exp_mem = jnp.exp(score_mem - row_max)
            totals = lax.optimization_barrier(jnp.sum(exp_loc, -1, keepdims=True)) + lax.optimization_barrier(jnp.sum(exp_mem, -1, keepdims=True))
            prob_loc = exp_loc / totals
            prob_mem = exp_mem / totals
            weight_loc = rounded(prob_loc)
            weight_mem = rounded(prob_mem)
            attended = jnp.einsum('hij,jhd->ihd', weight_loc, local_v) + jnp.einsum('hij,jhd->ihd', weight_mem, read_v)
            deltas = lax.optimization_barrier(jnp.sum(grad_b * attended, -1)).T[..., None]
            dprob_loc = jnp.einsum('ihd,jhd->hij', grad_b, local_v)
            dprob_mem = jnp.einsum('ihd,jhd->hij', grad_b, read_v)
            dscore_loc = rounded(prob_loc * (dprob_loc - deltas))
            dscore_mem = rounded(prob_mem * (dprob_mem - deltas))
            grad_query = (jnp.einsum('hij,jhd->ihd', dscore_loc, local_k) + jnp.einsum('hij,jhd->ihd', dscore_mem, read_k)) * scaling
            dkey_loc = jnp.einsum('hij,ihd->jhd', dscore_loc, query_b) * scaling
            dvalue_loc = jnp.einsum('hij,ihd->jhd', weight_loc, grad_b)
            dkey_mem = rounded(jnp.einsum('hij,ihd->jhd', dscore_mem, query_b) * scaling).reshape(READS, BLOCK, group_width)
            dvalue_mem = rounded(jnp.einsum('hij,ihd->jhd', weight_mem, grad_b)).reshape(READS, BLOCK, group_width)
            acc_k = lax.dynamic_update_slice_in_dim(acc_k, lax.dynamic_slice_in_dim(acc_k, first, win_span, 0) + dkey_loc.reshape(win_span, group_width), first, 0)
            acc_v = lax.dynamic_update_slice_in_dim(acc_v, lax.dynamic_slice_in_dim(acc_v, first, win_span, 0) + dvalue_loc.reshape(win_span, group_width), first, 0)
            mem_k = mem_k.at[which].add(dkey_mem)
            mem_v = mem_v.at[which].add(dvalue_mem)
            return ((acc_k, acc_v, mem_k, mem_v), grad_query.reshape(BLOCK, group_width).astype(jnp.bfloat16))
        init = (jnp.zeros((TOKENS + WINDOW, group_width), jnp.float32), jnp.zeros((TOKENS + WINDOW, group_width), jnp.float32), jnp.zeros((MEMBLOCKS, BLOCK, group_width), jnp.float32), jnp.zeros((MEMBLOCKS, BLOCK, group_width), jnp.float32))
        finals, grad_q = lax.scan(step, init, jnp.arange(QBLOCKS, dtype=jnp.int32))
        acc_k, acc_v, mem_k, mem_v = finals
        return (grad_q.reshape(TOKENS, group_width), acc_k[WINDOW:].astype(jnp.bfloat16), acc_v[WINDOW:].astype(jnp.bfloat16), mem_k.reshape(MEMTOK, group_width).astype(jnp.bfloat16), mem_v.reshape(MEMTOK, group_width).astype(jnp.bfloat16))
    stacked = lax.map(one_group, jnp.arange(HEAD_GROUP_COUNT, dtype=jnp.int32))

    def merge_heads(per_group):
        return jnp.transpose(per_group, (1, 0, 2)).reshape(per_group.shape[1], HEAD_GROUP_COUNT * group_width)
    return (merge_heads(stacked[0]), merge_heads(stacked[1]), merge_heads(stacked[2]), merge_heads(stacked[3]), merge_heads(stacked[4]))
```

```python
import functools
import math

import jax
import jax.numpy as jnp
from jax import lax
from jax.experimental import pallas as pl
from jax.experimental.pallas import tpu as pltpu
from jax.sharding import Mesh
from jax.sharding import PartitionSpec as P

HEAD_DIM = 128
GROUP_HEADS = 3
BLOCK = 64
READS = 4
WINDOW = 512
TILE = 128
MASKED = -1e30
SCALE = 1.0 / math.sqrt(HEAD_DIM)


def dot(a, b, contract):
    return lax.dot_general(a, b, ((contract[:1], contract[1:]), ((), ())), preferred_element_type=jnp.float32)


def attention_kernel(parts, slots_ref, reads_ref, start_ref, *refs):
    q_ref, do_ref, k_ref, v_ref, kt_ref, vt_ref = refs[:6]
    refs = refs[6:]
    ck_refs, cv_refs, refs = refs[:parts], refs[parts : 2 * parts], refs[2 * parts :]
    dq_ref, dk_ref, dv_ref, dkt_ref, dvt_ref = refs[:5]
    refs = refs[5:]
    gk_refs, gv_refs, refs = refs[:parts], refs[parts : 2 * parts], refs[2 * parts :]
    kx, vx, dkx, dvx = refs[:4]
    if parts > 1:
        ckx, cvx, gkx, gvx = refs[4:]
    else:
        ckx, cvx, gkx, gvx = ck_refs[0], cv_refs[0], gk_refs[0], gv_refs[0]
    rows = q_ref.shape[0]
    span = WINDOW + TILE
    group = pl.program_id(0) // GROUP_HEADS

    kx[:WINDOW] = kt_ref[...]
    kx[WINDOW:] = k_ref[...]
    vx[:WINDOW] = vt_ref[...]
    vx[WINDOW:] = v_ref[...]
    dkx[...] = jnp.zeros_like(dkx)
    dvx[...] = jnp.zeros_like(dvx)
    gkx[...] = jnp.zeros_like(gkx)
    gvx[...] = jnp.zeros_like(gvx)
    if parts > 1:
        part_rows = ck_refs[0].shape[0]
        for p in range(parts):
            ckx[p * part_rows : (p + 1) * part_rows] = ck_refs[p][...]
            cvx[p * part_rows : (p + 1) * part_rows] = cv_refs[p][...]

    key_at = lax.broadcasted_iota(jnp.int32, (TILE, TILE), 0)
    query_at = lax.broadcasted_iota(jnp.int32, (TILE, TILE), 1)
    first_half = lax.broadcasted_iota(jnp.int32, (1, TILE), 1) < BLOCK
    first_rows = lax.broadcasted_iota(jnp.int32, (TILE, 1), 0) < BLOCK
    at_start = start_ref[0]

    def tile(t, carry):
        at = pl.multiple_of(t * TILE, TILE)
        q = q_ref[pl.ds(at, TILE)]
        do = do_ref[pl.ds(at, TILE)]
        k_loc = kx[pl.ds(at, span)]
        v_loc = vx[pl.ds(at, span)]
        places = []
        k_mem, v_mem = [], []
        for b in range(TILE // BLOCK):
            block = (group * (rows // BLOCK) + t * (TILE // BLOCK) + b) * READS
            where = [pl.multiple_of(slots_ref[reads_ref[block + r]] * BLOCK, BLOCK) for r in range(READS)]
            places.append(where)
            k_mem.append(jnp.concatenate([ckx[pl.ds(w, BLOCK)] for w in where], 0))
            v_mem.append(jnp.concatenate([cvx[pl.ds(w, BLOCK)] for w in where], 0))

        s_loc = dot(k_loc, q, (1, 1))
        s_mem = jnp.where(first_half, dot(k_mem[0], q, (1, 1)), dot(k_mem[1], q, (1, 1)))
        pieces = []
        for c in range(span // TILE):
            piece = s_loc[c * TILE : (c + 1) * TILE]
            if c < span // TILE - 1:
                before = (at_start > 0) & (at + c * TILE < WINDOW)
                piece = piece + jnp.where(before, MASKED, 0.0)
            else:
                piece = jnp.where(key_at <= query_at, piece, MASKED)
            if c == 0:
                piece = jnp.where(key_at >= query_at, piece, MASKED)
            pieces.append(piece)
        s_loc = jnp.concatenate(pieces, 0)
        top = jnp.maximum(jnp.max(s_loc, 0, keepdims=True), jnp.max(s_mem, 0, keepdims=True))
        unit = SCALE * math.log2(math.e)
        e_loc = jnp.exp2((s_loc - top) * unit)
        e_mem = jnp.exp2((s_mem - top) * unit)
        total = jnp.sum(e_loc, 0, keepdims=True) + jnp.sum(e_mem, 0, keepdims=True)
        inverse = 1.0 / total
        p_loc = e_loc * inverse
        p_mem = e_mem * inverse
        w_loc = p_loc.astype(jnp.bfloat16)
        w_mem = p_mem.astype(jnp.bfloat16)
        dp_loc = dot(v_loc, do, (1, 1))
        dp_mem = jnp.where(first_half, dot(v_mem[0], do, (1, 1)), dot(v_mem[1], do, (1, 1)))
        delta = jnp.sum(w_loc.astype(jnp.float32) * dp_loc, 0, keepdims=True) + jnp.sum(
            w_mem.astype(jnp.float32) * dp_mem, 0, keepdims=True
        )
        ds_loc = (p_loc * (dp_loc - delta)).astype(jnp.bfloat16)
        ds_mem = (p_mem * (dp_mem - delta)).astype(jnp.bfloat16)

        dq_mem = jnp.where(first_rows, dot(ds_mem, k_mem[0], (0, 0)), dot(ds_mem, k_mem[1], (0, 0)))
        dq_ref[pl.ds(at, TILE)] = ((dot(ds_loc, k_loc, (0, 0)) + dq_mem) * SCALE).astype(dq_ref.dtype)
        dkx[pl.ds(at, span)] += dot(ds_loc, q, (1, 0))
        dvx[pl.ds(at, span)] += dot(w_loc, do, (1, 0))
        zero = jnp.zeros_like(q)
        q_two = jnp.concatenate([jnp.where(first_rows, q, zero), jnp.where(first_rows, zero, q)], 1)
        do_two = jnp.concatenate([jnp.where(first_rows, do, zero), jnp.where(first_rows, zero, do)], 1)
        read_k = (dot(ds_mem, q_two, (1, 0)) * SCALE).astype(jnp.bfloat16).astype(jnp.float32)
        read_v = dot(w_mem, do_two, (1, 0)).astype(jnp.bfloat16).astype(jnp.float32)
        for b in range(TILE // BLOCK):
            for r in range(READS):
                here = (slice(r * BLOCK, (r + 1) * BLOCK), slice(b * HEAD_DIM, (b + 1) * HEAD_DIM))
                gkx[pl.ds(places[b][r], BLOCK)] += read_k[here]
                gvx[pl.ds(places[b][r], BLOCK)] += read_v[here]
        return carry

    lax.fori_loop(0, rows // TILE, tile, 0)
    dkt_ref[...] = (dkx[:WINDOW] * SCALE).astype(dkt_ref.dtype)
    dvt_ref[...] = dvx[:WINDOW].astype(dvt_ref.dtype)
    dk_ref[...] = dkx[WINDOW:] * SCALE
    dv_ref[...] = dvx[WINDOW:]
    if parts > 1:
        for p in range(parts):
            gk_refs[p][...] = gkx[p * part_rows : (p + 1) * part_rows].astype(gk_refs[p].dtype)
            gv_refs[p][...] = gvx[p * part_rows : (p + 1) * part_rows].astype(gv_refs[p].dtype)


def attention(slots, reads, start, qd, kv, tails, cache_k, cache_v):
    rows, width = qd.shape[0], qd.shape[1] // 2
    heads = width // HEAD_DIM
    parts = len(cache_k)
    part_rows = cache_k[0].shape[0]

    def column(height, offset=0):
        return pl.BlockSpec((height, HEAD_DIM), lambda h, *_: (0, h + offset))

    bf16, f32 = jnp.bfloat16, jnp.float32
    kinds = [f32] + [bf16] * (parts - 1)
    shape = jax.ShapeDtypeStruct
    scratch = [
        pltpu.VMEM((WINDOW + rows, HEAD_DIM), bf16),
        pltpu.VMEM((WINDOW + rows, HEAD_DIM), bf16),
        pltpu.VMEM((WINDOW + rows, HEAD_DIM), f32),
        pltpu.VMEM((WINDOW + rows, HEAD_DIM), f32),
    ]
    if parts > 1:
        scratch += [pltpu.VMEM((parts * part_rows, HEAD_DIM), kind) for kind in (bf16, bf16, f32, f32)]
    pairs = heads * rows * (WINDOW + TILE + 2 * READS * BLOCK)
    outs = pl.pallas_call(
        functools.partial(attention_kernel, parts),
        grid_spec=pltpu.PrefetchScalarGridSpec(
            num_scalar_prefetch=3,
            grid=(heads,),
            in_specs=[
                column(rows),
                column(rows, heads),
                column(rows),
                column(rows, heads),
                column(WINDOW),
                column(WINDOW, heads),
            ]
            + [column(part_rows)] * (2 * parts),
            out_specs=[column(rows)] * 3 + [column(WINDOW)] * 2 + [column(part_rows)] * (2 * parts),
            scratch_shapes=scratch,
        ),
        out_shape=[shape((rows, width), bf16), shape((rows, width), f32), shape((rows, width), f32)]
        + [shape((WINDOW, width), bf16)] * 2
        + [shape((part_rows, width), kind) for kind in kinds] * 2,
        compiler_params=pltpu.CompilerParams(vmem_limit_bytes=56 * 2**20),
        cost_estimate=pl.CostEstimate(
            flops=10 * pairs * HEAD_DIM, bytes_accessed=heads * part_rows * parts * 1400, transcendentals=pairs
        ),
        name="attention",
    )(slots, reads, start, qd, qd, kv, kv, tails, tails, *cache_k, *cache_v)
    return outs[:5], outs[5 : 5 + parts], outs[5 + parts :]


def per_device(queries, keys_local, values_local, cache_keys, cache_values, block_map, retrieved, out_grad):
    chips, zs = lax.axis_size("chip"), lax.axis_size("head")
    chip, core = lax.axis_index("chip"), lax.axis_index("core")
    rows, features = queries.shape
    blk_dev = cache_keys.shape[0] // BLOCK
    groups = retrieved.shape[1]
    split = 2 if groups % 2 == 0 else 1
    head_axes = ("core", "head") if split == 2 else ("head",)
    token_axes = ("chip",) if split == 2 else ("chip", "core")
    peers = split * zs
    width = features // peers
    tokens = rows * peers
    token_parts = chips if split == 2 else 2 * chips
    token_index = lax.axis_index(token_axes)
    relay = split == 2 and chips == 4
    seq_parts = min(8, 2 * chips) * cache_keys.shape[0] // tokens

    def to_heads(arrays):
        packed = [
            a.reshape(rows, zs, split, width).transpose(2, 1, 0, 3).reshape(peers, rows, width) for a in arrays
        ]
        packed = jnp.concatenate(packed, 2)
        moved = lax.all_to_all(packed, head_axes, split_axis=0, concat_axis=0, tiled=True)
        return moved.reshape(tokens, len(arrays) * width)

    def to_tokens(array):
        moved = lax.all_to_all(
            array.reshape(peers, rows, width), head_axes, split_axis=0, concat_axis=0, tiled=True
        )
        return moved.reshape(split, zs, rows, width).transpose(2, 1, 0, 3).reshape(rows, features)

    def other_core(array):
        return lax.ppermute(array, "core", [(0, 1), (1, 0)])

    def other_chip(array, by):
        return lax.ppermute(array, "chip", [(i, i ^ by) for i in range(chips)])

    def half(array, which):
        return lax.dynamic_slice_in_dim(array, which * width, width, 1)

    if split == 2:
        cache_k, cache_v = (
            jnp.concatenate([half(a, core), other_core(half(a, 1 - core))], 0) for a in (cache_keys, cache_values)
        )
        theirs = other_core(retrieved)
        ids = jnp.where(core == 0, jnp.stack([retrieved, theirs]), jnp.stack([theirs, retrieved]))
        ids = ids.reshape((-1,) + retrieved.shape[1:])
        ids = lax.dynamic_slice_in_dim(ids, core * (groups // 2), groups // 2, 1)
    else:
        cache_k, cache_v, ids = cache_keys, cache_values, retrieved
    reads = jnp.transpose(ids, (1, 0, 2)).reshape(-1)
    owner, local = block_map // blk_dev, block_map % blk_dev
    owner_chip, owner_core = owner // 2, owner % 2
    if relay:
        owner_chip = owner_chip ^ chip
    if split == 2:
        owner_core = owner_core ^ core
    slots = ((owner_chip * 2 + owner_core) * blk_dev + local).astype(jnp.int32)
    start = (token_index % seq_parts == 0).astype(jnp.int32).reshape(1)

    if relay:
        k_y = other_chip(cache_k, 2)
        v_x = other_chip(cache_v, 1)
        k_x = other_chip(cache_k, 1)
        v_y = other_chip(cache_v, 2)
        all_k = [cache_k, k_x, k_y, other_chip(k_y, 1)]
        all_v = [cache_v, v_x, v_y, other_chip(v_x, 2)]
    else:
        all_k, all_v = ([lax.all_gather(a, token_axes, tiled=True)] for a in (cache_k, cache_v))

    kv = to_heads([keys_local, values_local])
    tails = lax.ppermute(kv[tokens - WINDOW :], token_axes, [(i, i + 1) for i in range(token_parts - 1)])
    qd = to_heads([queries, out_grad])
    (dq, dk, dv, dkt, dvt), gk, gv = attention(slots, reads, start, qd, kv, tails, all_k, all_v)

    back = [(i + 1, i) for i in range(token_parts - 1)]
    dkt, dvt = lax.ppermute((dkt, dvt), token_axes, back)

    def with_tail(own, tail):
        own = jnp.concatenate([own[: tokens - WINDOW], own[tokens - WINDOW :] + tail.astype(jnp.float32)], 0)
        return own.astype(jnp.bfloat16)

    if relay:
        bf16, f32 = jnp.bfloat16, jnp.float32
        k_far = other_chip(gk[3], 1)
        v_far = other_chip(gv[3], 2)
        k_x = other_chip(gk[1], 1)
        v_y = other_chip(gv[2], 2)
        k_y = other_chip((gk[2].astype(f32) + k_far.astype(f32)).astype(bf16), 2)
        v_x = other_chip((gv[1].astype(f32) + v_far.astype(f32)).astype(bf16), 1)
        sum_k = (gk[0] + k_x.astype(f32) + k_y.astype(f32)).astype(bf16)
        sum_v = (gv[0] + v_x.astype(f32) + v_y.astype(f32)).astype(bf16)
    else:
        sum_k, sum_v = (
            lax.psum_scatter(g[0], token_axes, scatter_dimension=0, tiled=True).astype(jnp.bfloat16) for g in (gk, gv)
        )
    if split == 2:
        own_rows = sum_k.shape[0] // 2

        def to_owner(total):
            mine, recv = total[:own_rows], other_core(total[own_rows:])
            return jnp.where(core == 0, jnp.concatenate([mine, recv], 1), jnp.concatenate([recv, mine], 1))

        sum_k, sum_v = to_owner(sum_k), to_owner(sum_v)

    out_q = to_tokens(dq)
    out_k = to_tokens(with_tail(dk, dkt))
    out_v = to_tokens(with_tail(dv, dvt))
    return out_q, out_k, out_v, sum_k, sum_v


def solution(mesh):
    shape = mesh.shape
    fine = Mesh(mesh.devices.reshape(shape["mem"] // 2, 2, shape["head"]), ("chip", "core", "head"))
    by_token = P(("chip", "core", "head"), None)
    by_block = P(("chip", "core"), "head")
    return jax.shard_map(
        per_device,
        mesh=fine,
        in_specs=(
            by_token,
            by_token,
            by_token,
            by_block,
            by_block,
            P(),
            P(("chip", "core"), "head", None),
            by_token,
        ),
        out_specs=(by_token, by_token, by_token, by_block, by_block),
        check_vma=False,
    )
```

```python
import functools
import math

import jax
import jax.numpy as jnp
from jax import lax
from jax.experimental import pallas as pl
from jax.experimental.pallas import tpu as pltpu
from jax.sharding import Mesh
from jax.sharding import PartitionSpec as P

HEAD_DIM = 128
GROUP_HEADS = 3
BLOCK = 64
READS = 4
WINDOW = 512
TILE = 128
MASKED = -1e30
SCALE = 1.0 / math.sqrt(HEAD_DIM)


def dot(a, b, contract):
    return lax.dot_general(a, b, ((contract[:1], contract[1:]), ((), ())), preferred_element_type=jnp.float32)


def after(values, others):
    return lax.optimization_barrier((values, others))[0]


def pack(first, second, peers, split, stages):
    rows, features = first.shape
    width = features // (peers * stages)
    zs = peers // split

    def body(a_ref, b_ref, *outs):
        for s in range(stages):
            for c in range(split):
                at = (c * stages + s) * width
                outs[s][c, 0, :, :width] = a_ref[:, at : at + width]
                outs[s][c, 0, :, width:] = b_ref[:, at : at + width]

    return pl.pallas_call(
        body,
        grid=(zs,),
        in_specs=[pl.BlockSpec((rows, features // zs), lambda z: (0, z))] * 2,
        out_specs=[pl.BlockSpec((split, 1, rows, 2 * width), lambda z: (0, z, 0, 0))] * stages,
        out_shape=[jax.ShapeDtypeStruct((split, zs, rows, 2 * width), first.dtype)] * stages,
        cost_estimate=pl.CostEstimate(flops=0, bytes_accessed=8 * rows * features, transcendentals=0),
        name="pack",
    )(first, second)


def unpack(moved, width, offset):
    stages = len(moved)
    split, zs, rows, _ = moved[0].shape

    def body(*refs):
        for s in range(stages):
            for c in range(split):
                at = (c * stages + s) * width
                refs[-1][:, at : at + width] = refs[s][c, 0]

    return pl.pallas_call(
        body,
        grid=(zs,),
        in_specs=[pl.BlockSpec((split, 1, rows, width), lambda z: (0, z, 0, offset))] * stages,
        out_specs=pl.BlockSpec((rows, split * stages * width), lambda z: (0, z)),
        out_shape=jax.ShapeDtypeStruct((rows, zs * split * stages * width), moved[0].dtype),
        cost_estimate=pl.CostEstimate(flops=0, bytes_accessed=4 * rows * zs * split * stages * width, transcendentals=0),
        name="unpack",
    )(*moved)


def finish_late(dk, dv, dk_late, dv_late, back_k, back_v):
    tokens, width = dk.shape
    early = tokens - WINDOW

    def body(k_ref, v_ref, k_late_ref, v_late_ref, back_k_ref, back_v_ref, out_ref):
        if early:
            out_ref[:early, :width] = k_ref[:early]
            out_ref[:early, width:] = v_ref[:early]
        out_ref[early:, :width] = (k_late_ref[...] + back_k_ref[...].astype(jnp.float32)).astype(out_ref.dtype)
        out_ref[early:, width:] = (v_late_ref[...] + back_v_ref[...].astype(jnp.float32)).astype(out_ref.dtype)

    return pl.pallas_call(
        body,
        out_shape=jax.ShapeDtypeStruct((tokens, 2 * width), dk.dtype),
        compiler_params=pltpu.CompilerParams(vmem_limit_bytes=32 * 2**20),
        cost_estimate=pl.CostEstimate(flops=0, bytes_accessed=12 * tokens * width, transcendentals=0),
        name="finish_late",
    )(dk, dv, dk_late, dv_late, back_k, back_v)


def attention_kernel(parts, slots_ref, reads_ref, start_ref, *refs):
    q_ref, do_ref, k_ref, v_ref, kt_ref, vt_ref = refs[:6]
    refs = refs[6:]
    ck_refs, cv_refs, refs = refs[:parts], refs[parts : 2 * parts], refs[2 * parts :]
    dq_ref, dk_ref, dv_ref, dk_late_ref, dv_late_ref, dkt_ref, dvt_ref = refs[:7]
    refs = refs[7:]
    gk_refs, gv_refs, refs = refs[:parts], refs[parts : 2 * parts], refs[2 * parts :]
    kx, vx, dkx, dvx = refs[:4]
    if parts > 1:
        ckx, cvx, gkx, gvx = refs[4:]
    else:
        ckx, cvx, gkx, gvx = ck_refs[0], cv_refs[0], gk_refs[0], gv_refs[0]
    rows = q_ref.shape[0]
    span = WINDOW + TILE
    group = pl.program_id(0) // GROUP_HEADS

    kx[:WINDOW] = kt_ref[...]
    kx[WINDOW:] = k_ref[...]
    vx[:WINDOW] = vt_ref[...]
    vx[WINDOW:] = v_ref[...]
    dkx[...] = jnp.zeros_like(dkx)
    dvx[...] = jnp.zeros_like(dvx)
    gkx[...] = jnp.zeros_like(gkx)
    gvx[...] = jnp.zeros_like(gvx)
    if parts > 1:
        part_rows = ck_refs[0].shape[0]
        for p in range(parts):
            ckx[p * part_rows : (p + 1) * part_rows] = ck_refs[p][...]
            cvx[p * part_rows : (p + 1) * part_rows] = cv_refs[p][...]

    key_at = lax.broadcasted_iota(jnp.int32, (TILE, TILE), 0)
    query_at = lax.broadcasted_iota(jnp.int32, (TILE, TILE), 1)
    first_half = lax.broadcasted_iota(jnp.int32, (1, TILE), 1) < BLOCK
    first_rows = lax.broadcasted_iota(jnp.int32, (TILE, 1), 0) < BLOCK
    at_start = start_ref[0]

    def tile(t, carry):
        at = pl.multiple_of(t * TILE, TILE)
        q = q_ref[pl.ds(at, TILE)]
        do = do_ref[pl.ds(at, TILE)]
        k_loc = kx[pl.ds(at, span)]
        v_loc = vx[pl.ds(at, span)]
        places = []
        k_mem, v_mem = [], []
        for b in range(TILE // BLOCK):
            block = (group * (rows // BLOCK) + t * (TILE // BLOCK) + b) * READS
            where = [pl.multiple_of(slots_ref[reads_ref[block + r]] * BLOCK, BLOCK) for r in range(READS)]
            places.append(where)
            k_mem.append(jnp.concatenate([ckx[pl.ds(w, BLOCK)] for w in where], 0))
            v_mem.append(jnp.concatenate([cvx[pl.ds(w, BLOCK)] for w in where], 0))

        s_loc = dot(k_loc, q, (1, 1))
        s_mem = jnp.where(first_half, dot(k_mem[0], q, (1, 1)), dot(k_mem[1], q, (1, 1)))
        pieces = []
        for c in range(span // TILE):
            piece = s_loc[c * TILE : (c + 1) * TILE]
            if c < span // TILE - 1:
                before = (at_start > 0) & (at + c * TILE < WINDOW)
                piece = piece + jnp.where(before, MASKED, 0.0)
            else:
                piece = jnp.where(key_at <= query_at, piece, MASKED)
            if c == 0:
                piece = jnp.where(key_at >= query_at, piece, MASKED)
            pieces.append(piece)
        s_loc = jnp.concatenate(pieces, 0)
        top = jnp.maximum(jnp.max(s_loc, 0, keepdims=True), jnp.max(s_mem, 0, keepdims=True))
        unit = SCALE * math.log2(math.e)
        e_loc = jnp.exp2((s_loc - top) * unit)
        e_mem = jnp.exp2((s_mem - top) * unit)
        total = jnp.sum(e_loc, 0, keepdims=True) + jnp.sum(e_mem, 0, keepdims=True)
        inverse = 1.0 / total
        p_loc = e_loc * inverse
        p_mem = e_mem * inverse
        w_loc = p_loc.astype(jnp.bfloat16)
        w_mem = p_mem.astype(jnp.bfloat16)
        dp_loc = dot(v_loc, do, (1, 1))
        dp_mem = jnp.where(first_half, dot(v_mem[0], do, (1, 1)), dot(v_mem[1], do, (1, 1)))
        delta = jnp.sum(w_loc.astype(jnp.float32) * dp_loc, 0, keepdims=True) + jnp.sum(
            w_mem.astype(jnp.float32) * dp_mem, 0, keepdims=True
        )
        ds_loc = (p_loc * (dp_loc - delta)).astype(jnp.bfloat16)
        ds_mem = (p_mem * (dp_mem - delta)).astype(jnp.bfloat16)

        dq_mem = jnp.where(first_rows, dot(ds_mem, k_mem[0], (0, 0)), dot(ds_mem, k_mem[1], (0, 0)))
        dq_ref[pl.ds(at, TILE)] = ((dot(ds_loc, k_loc, (0, 0)) + dq_mem) * SCALE).astype(dq_ref.dtype)
        dkx[pl.ds(at, span)] += dot(ds_loc, q, (1, 0))
        dvx[pl.ds(at, span)] += dot(w_loc, do, (1, 0))
        zero = jnp.zeros_like(q)
        q_two = jnp.concatenate([jnp.where(first_rows, q, zero), jnp.where(first_rows, zero, q)], 1)
        do_two = jnp.concatenate([jnp.where(first_rows, do, zero), jnp.where(first_rows, zero, do)], 1)
        read_k = (dot(ds_mem, q_two, (1, 0)) * SCALE).astype(jnp.bfloat16).astype(jnp.float32)
        read_v = dot(w_mem, do_two, (1, 0)).astype(jnp.bfloat16).astype(jnp.float32)
        for b in range(TILE // BLOCK):
            for r in range(READS):
                here = (slice(r * BLOCK, (r + 1) * BLOCK), slice(b * HEAD_DIM, (b + 1) * HEAD_DIM))
                gkx[pl.ds(places[b][r], BLOCK)] += read_k[here]
                gvx[pl.ds(places[b][r], BLOCK)] += read_v[here]
        return carry

    lax.fori_loop(0, rows // TILE, tile, 0)
    dkt_ref[...] = (dkx[:WINDOW] * SCALE).astype(dkt_ref.dtype)
    dvt_ref[...] = dvx[:WINDOW].astype(dvt_ref.dtype)
    dk_ref[...] = (dkx[WINDOW:] * SCALE).astype(dk_ref.dtype)
    dv_ref[...] = dvx[WINDOW:].astype(dv_ref.dtype)
    dk_late_ref[...] = dkx[rows:] * SCALE
    dv_late_ref[...] = dvx[rows:]
    if parts > 1:
        for p in range(parts):
            gk_refs[p][...] = gkx[p * part_rows : (p + 1) * part_rows].astype(gk_refs[p].dtype)
            gv_refs[p][...] = gvx[p * part_rows : (p + 1) * part_rows].astype(gv_refs[p].dtype)


def attention(slots, reads, start, qd, kv, tails, cache_k, cache_v):
    rows, width = qd.shape[0], qd.shape[1] // 2
    heads = width // HEAD_DIM
    parts = len(cache_k)
    part_rows = cache_k[0].shape[0]

    def column(height, offset=0):
        return pl.BlockSpec((height, HEAD_DIM), lambda h, *_: (0, h + offset))

    bf16, f32 = jnp.bfloat16, jnp.float32
    kinds = [f32] + [bf16] * (parts - 1)
    shape = jax.ShapeDtypeStruct
    scratch = [
        pltpu.VMEM((WINDOW + rows, HEAD_DIM), bf16),
        pltpu.VMEM((WINDOW + rows, HEAD_DIM), bf16),
        pltpu.VMEM((WINDOW + rows, HEAD_DIM), f32),
        pltpu.VMEM((WINDOW + rows, HEAD_DIM), f32),
    ]
    if parts > 1:
        scratch += [pltpu.VMEM((parts * part_rows, HEAD_DIM), kind) for kind in (bf16, bf16, f32, f32)]
    pairs = heads * rows * (WINDOW + TILE + 2 * READS * BLOCK)
    outs = pl.pallas_call(
        functools.partial(attention_kernel, parts),
        grid_spec=pltpu.PrefetchScalarGridSpec(
            num_scalar_prefetch=3,
            grid=(heads,),
            in_specs=[
                column(rows),
                column(rows, heads),
                column(rows),
                column(rows, heads),
                column(WINDOW),
                column(WINDOW, heads),
            ]
            + [column(part_rows)] * (2 * parts),
            out_specs=[column(rows)] * 3 + [column(WINDOW)] * 4 + [column(part_rows)] * (2 * parts),
            scratch_shapes=scratch,
        ),
        out_shape=[shape((rows, width), bf16)] * 3
        + [shape((WINDOW, width), f32)] * 2
        + [shape((WINDOW, width), bf16)] * 2
        + [shape((part_rows, width), kind) for kind in kinds] * 2,
        compiler_params=pltpu.CompilerParams(vmem_limit_bytes=56 * 2**20),
        cost_estimate=pl.CostEstimate(
            flops=10 * pairs * HEAD_DIM, bytes_accessed=heads * part_rows * parts * 1400, transcendentals=pairs
        ),
        name="attention",
    )(slots, reads, start, qd, qd, kv, kv, tails, tails, *cache_k, *cache_v)
    return outs[:7], outs[7 : 7 + parts], outs[7 + parts :]


def per_device(queries, keys_local, values_local, cache_keys, cache_values, block_map, retrieved, out_grad):
    chips, zs = lax.axis_size("chip"), lax.axis_size("head")
    chip, core = lax.axis_index("chip"), lax.axis_index("core")
    rows, features = queries.shape
    blk_dev = cache_keys.shape[0] // BLOCK
    groups = retrieved.shape[1]
    split = 2 if groups % 2 == 0 else 1
    head_axes = ("core", "head") if split == 2 else ("head",)
    token_axes = ("chip",) if split == 2 else ("chip", "core")
    peers = split * zs
    stages = groups // split
    width = features // (peers * stages)
    tokens = rows * peers
    token_parts = chips if split == 2 else 2 * chips
    token_index = lax.axis_index(token_axes)
    relay = split == 2 and chips == 4
    seq_parts = min(8, 2 * chips) * cache_keys.shape[0] // tokens
    bf16, f32 = jnp.bfloat16, jnp.float32

    def exchange(array):
        return lax.all_to_all(array, head_axes, split_axis=0, concat_axis=0, tiled=True)

    def to_heads(packed):
        moved = exchange(packed.reshape(peers, rows, 2 * width))
        return moved.reshape(tokens, 2 * width)

    def to_tokens(array):
        moved = exchange(array.reshape(peers, rows, array.shape[1]))
        return moved.reshape(split, zs, rows, array.shape[1])

    def other_core(array):
        return lax.ppermute(array, "core", [(0, 1), (1, 0)])

    def other_chip(array, by):
        return lax.ppermute(array, "chip", [(i, i ^ by) for i in range(chips)])

    def columns(array, which, stage):
        return lax.dynamic_slice_in_dim(array, (which * stages + stage) * width, width, 1)

    def own_cache(array, stage):
        if split == 1:
            return array
        return jnp.concatenate([columns(array, core, stage), other_core(columns(array, 1 - core, stage))], 0)

    ids = retrieved
    if split == 2:
        theirs = other_core(retrieved)
        ids = jnp.where(core == 0, jnp.stack([retrieved, theirs]), jnp.stack([theirs, retrieved]))
        ids = ids.reshape((-1,) + retrieved.shape[1:])
        ids = lax.dynamic_slice_in_dim(ids, core * stages, stages, 1)
    reads = jnp.transpose(ids, (1, 0, 2)).reshape(stages, -1)
    owner, local = block_map // blk_dev, block_map % blk_dev
    owner_chip, owner_core = owner // 2, owner % 2
    if relay:
        owner_chip = owner_chip ^ chip
    if split == 2:
        owner_core = owner_core ^ core
    slots = ((owner_chip * 2 + owner_core) * blk_dev + local).astype(jnp.int32)
    start = (token_index % seq_parts == 0).astype(jnp.int32).reshape(1)
    forth = [(i, i + 1) for i in range(token_parts - 1)]
    back = [(i + 1, i) for i in range(token_parts - 1)]

    def gather_near(k, v):
        if not relay:
            return ()
        return other_chip(k, 1), other_chip(k, 2), other_chip(v, 1), other_chip(v, 2)

    def gather_far(k, v, near):
        if not relay:
            return [lax.all_gather(k, token_axes, tiled=True)], [lax.all_gather(v, token_axes, tiled=True)]
        k_x, k_y, v_x, v_y = near
        return [k, k_x, k_y, other_chip(k_y, 1)], [v, v_x, v_y, other_chip(v_x, 2)]

    def reduce_far(gk, gv):
        return (other_chip(gk[3], 1), other_chip(gv[3], 2)) if relay else ()

    def reduce_near(gk, gv, far):
        if not relay:
            return [lax.psum_scatter(g[0], token_axes, scatter_dimension=0, tiled=True).astype(bf16) for g in (gk, gv)]
        k_y = other_chip((gk[2].astype(f32) + far[0].astype(f32)).astype(bf16), 2)
        v_x = other_chip((gv[1].astype(f32) + far[1].astype(f32)).astype(bf16), 1)
        k_x = other_chip(gk[1], 1)
        v_y = other_chip(gv[2], 2)
        return [(own[0] + x.astype(f32) + y.astype(f32)).astype(bf16) for own, x, y in ((gk, k_x, k_y), (gv, v_x, v_y))]

    def to_owner(totals):
        if split == 1:
            return totals[0]
        own_rows = totals[0].shape[0] // 2
        mine = jnp.concatenate([t[:own_rows] for t in totals], 1)
        recv = jnp.concatenate([other_core(t[own_rows:]) for t in totals], 1)
        return jnp.where(core == 0, jnp.concatenate([mine, recv], 1), jnp.concatenate([recv, mine], 1))

    kv = pack(keys_local, values_local, peers, split, stages)
    qd = pack(queries, out_grad, peers, split, stages)
    done = ()
    ready = []
    for s in range(stages):
        k, v, kv_s = after((own_cache(cache_keys, s), own_cache(cache_values, s), kv[s]), done)
        near = gather_near(k, v)
        kv_s = to_heads(kv_s)
        qd_s, kv_s, near = after((qd[s], kv_s, near), ())
        far = gather_far(k, v, near)
        tails = lax.ppermute(kv_s[tokens - WINDOW :], token_axes, forth)
        qd_s = to_heads(qd_s)
        done = (tails, qd_s, far)
        ready.append((qd_s, kv_s, tails, *far))
    grads = []
    moved_q, moved_kv, totals_k, totals_v = [], [], [], []
    for s in range(stages):
        grads.append(attention(slots, reads[s], start, *ready[s]))
    done = ready[-1]
    for s in range(stages):
        (dq, dk, dv, dk_late, dv_late, dkt, dvt), gk, gv = after(grads[s], done)
        back_k, back_v = lax.ppermute((dkt, dvt), token_axes, back)
        far = reduce_far(gk, gv)
        dq = to_tokens(dq)
        far, dq, dkv = after((far, dq, finish_late(dk, dv, dk_late, dv_late, back_k, back_v)), ())
        dkv = to_tokens(dkv)
        total_k, total_v = reduce_near(gk, gv, far)
        done = (dkv, total_k, total_v)
        moved_q.append(dq)
        moved_kv.append(dkv)
        totals_k.append(total_k)
        totals_v.append(total_v)
    return (
        unpack(moved_q, width, 0),
        unpack(moved_kv, width, 0),
        unpack(moved_kv, width, 1),
        to_owner(totals_k),
        to_owner(totals_v),
    )


def solution(mesh):
    shape = mesh.shape
    fine = Mesh(mesh.devices.reshape(shape["mem"] // 2, 2, shape["head"]), ("chip", "core", "head"))
    by_token = P(("chip", "core", "head"), None)
    by_block = P(("chip", "core"), "head")
    return jax.shard_map(
        per_device,
        mesh=fine,
        in_specs=(
            by_token,
            by_token,
            by_token,
            by_block,
            by_block,
            P(),
            P(("chip", "core"), "head", None),
            by_token,
        ),
        out_specs=(by_token, by_token, by_token, by_block, by_block),
        check_vma=False,
    )
```

```python
import functools
import math

import jax
import jax.numpy as jnp
from jax import lax
from jax.experimental import pallas as pl
from jax.experimental.pallas import tpu as pltpu
from jax.sharding import Mesh
from jax.sharding import PartitionSpec as P

HEAD_DIM = 128
GROUP_HEADS = 3
BLOCK = 64
READS = 4
WINDOW = 512
TILE = 128
MASKED = -1e30
UNROLL = 4
SCALE = 1.0 / math.sqrt(HEAD_DIM)


def dot(a, b, contract):
    return lax.dot_general(a, b, ((contract[:1], contract[1:]), ((), ())), preferred_element_type=jnp.float32)


def after(values, others):
    return lax.optimization_barrier((values, others))[0]


def moved_bytes(count):
    return pl.CostEstimate(flops=0, bytes_accessed=count, transcendentals=0)


def pack_tokens(arrays, split, zs, cuts):
    rows, features = arrays[0].shape
    group = features // (split * zs)
    count = len(arrays)

    def body(*refs):
        for out, (low, high) in zip(refs[count:], cuts):
            for c in range(split):
                for n in range(count):
                    out[c, 0, :, n * (high - low) : (n + 1) * (high - low)] = refs[n][:, c * group + low : c * group + high]

    widths = [count * (high - low) for low, high in cuts]
    return pl.pallas_call(
        body,
        grid=(zs,),
        in_specs=[pl.BlockSpec((rows, features // zs), lambda z: (0, z))] * count,
        out_specs=[pl.BlockSpec((split, 1, rows, w), lambda z: (0, z, 0, 0)) for w in widths],
        out_shape=[jax.ShapeDtypeStruct((split, zs, rows, w), arrays[0].dtype) for w in widths],
        cost_estimate=moved_bytes(4 * count * rows * features),
        name="pack_tokens",
    )(*arrays)


def unpack_tokens(moved, cuts, count):
    split, zs, rows, _ = moved[0].shape
    group = cuts[-1][1]

    def body(*refs):
        for ref, (low, high) in zip(refs, cuts):
            for c in range(split):
                for n in range(count):
                    refs[len(cuts) + n][:, c * group + low : c * group + high] = ref[
                        c, 0, :, n * (high - low) : (n + 1) * (high - low)
                    ]

    features = zs * split * group
    return pl.pallas_call(
        body,
        grid=(zs,),
        in_specs=[pl.BlockSpec((split, 1, rows, m.shape[3]), lambda z: (0, z, 0, 0)) for m in moved],
        out_specs=[pl.BlockSpec((rows, split * group), lambda z: (0, z))] * count,
        out_shape=[jax.ShapeDtypeStruct((rows, features), moved[0].dtype)] * count,
        cost_estimate=moved_bytes(4 * count * rows * features),
        name="unpack_tokens",
    )(*moved)


def pack_cache(cache_k, cache_v, order):
    rows, features = cache_k.shape
    parts = order.shape[0]
    group = features // parts

    def body(order_ref, k_ref, v_ref, *outs):
        for p in range(parts):

            @pl.when(pl.program_id(0) == p)
            def _(p=p):
                outs[p][:, :group] = k_ref[...]
                outs[p][:, group:] = v_ref[...]

    return pl.pallas_call(
        body,
        grid_spec=pltpu.PrefetchScalarGridSpec(
            num_scalar_prefetch=1,
            grid=(parts,),
            in_specs=[pl.BlockSpec((rows, group), lambda p, order: (0, order[p]))] * 2,
            out_specs=[pl.BlockSpec((rows, 2 * group), lambda p, order: (0, 0))] * parts,
        ),
        out_shape=[jax.ShapeDtypeStruct((rows, 2 * group), cache_k.dtype)] * parts,
        compiler_params=pltpu.CompilerParams(vmem_limit_bytes=32 * 2**20),
        cost_estimate=moved_bytes(8 * rows * features),
        name="pack_cache",
    )(order, cache_k, cache_v)


def sum_cores(mine_k, mine_v, recv_k, recv_v, parts):
    rows, width = mine_k.shape[0] // parts, mine_k.shape[1]

    def body(mine_k_ref, mine_v_ref, recv_k_ref, recv_v_ref, *outs):
        for p in range(parts):

            @pl.when(pl.program_id(0) == p)
            def _(p=p):
                outs[p][:, :width] = (mine_k_ref[...] + recv_k_ref[...]).astype(outs[p].dtype)
                outs[p][:, width:] = (mine_v_ref[...] + recv_v_ref[...]).astype(outs[p].dtype)

    return pl.pallas_call(
        body,
        grid=(parts,),
        in_specs=[pl.BlockSpec((rows, width), lambda p: (p, 0))] * 4,
        out_specs=[pl.BlockSpec((rows, 2 * width), lambda p: (0, 0))] * parts,
        out_shape=[jax.ShapeDtypeStruct((rows, 2 * width), jnp.bfloat16)] * parts,
        compiler_params=pltpu.CompilerParams(vmem_limit_bytes=32 * 2**20),
        cost_estimate=moved_bytes(20 * parts * rows * width),
        name="sum_cores",
    )(mine_k, mine_v, recv_k, recv_v)


def place_cache(stages, order, cuts):
    parts = order.shape[0]
    rows, group = stages[0][0].shape[0], cuts[-1][1]
    arrays = [a for stage in stages for a in stage]

    def body(order_ref, *refs):
        k_ref, v_ref = refs[len(arrays) :]
        for p in range(parts):

            @pl.when(pl.program_id(0) == p)
            def _(p=p):
                for s, (low, high) in enumerate(cuts):
                    k_ref[:, low:high] = refs[s * parts + p][:, : high - low]
                    v_ref[:, low:high] = refs[s * parts + p][:, high - low :]

    return pl.pallas_call(
        body,
        grid_spec=pltpu.PrefetchScalarGridSpec(
            num_scalar_prefetch=1,
            grid=(parts,),
            in_specs=[pl.BlockSpec(a.shape, lambda p, order: (0, 0)) for a in arrays],
            out_specs=[pl.BlockSpec((rows, group), lambda p, order: (0, order[p]))] * 2,
        ),
        out_shape=[jax.ShapeDtypeStruct((rows, parts * group), arrays[0].dtype)] * 2,
        compiler_params=pltpu.CompilerParams(vmem_limit_bytes=32 * 2**20),
        cost_estimate=moved_bytes(8 * rows * parts * group),
        name="place_cache",
    )(order, *arrays)


def finish_tokens(back_at, back_on, dq, dk, dv, back_k, back_v):
    tokens, width = dq.shape

    def body(back_at_ref, back_on_ref, dq_ref, dk_ref, dv_ref, back_k_ref, back_v_ref, out_ref):
        on = back_on_ref[pl.program_id(0)] > 0
        out_ref[:, :width] = dq_ref[...]
        out_ref[:, width : 2 * width] = (dk_ref[...] + jnp.where(on, back_k_ref[...], 0.0)).astype(out_ref.dtype)
        out_ref[:, 2 * width :] = (dv_ref[...] + jnp.where(on, back_v_ref[...], 0.0)).astype(out_ref.dtype)

    own = pl.BlockSpec((WINDOW, width), lambda j, at, on: (j, 0))
    back = pl.BlockSpec((WINDOW, width), lambda j, at, on: (at[j], 0))
    return pl.pallas_call(
        body,
        grid_spec=pltpu.PrefetchScalarGridSpec(
            num_scalar_prefetch=2,
            grid=(tokens // WINDOW,),
            in_specs=[own, own, own, back, back],
            out_specs=pl.BlockSpec((WINDOW, 3 * width), lambda j, at, on: (j, 0)),
        ),
        out_shape=jax.ShapeDtypeStruct((tokens, 3 * width), jnp.bfloat16),
        compiler_params=pltpu.CompilerParams(vmem_limit_bytes=32 * 2**20),
        cost_estimate=moved_bytes(24 * tokens * width),
        name="finish_tokens",
    )(back_at, back_on, dq, dk, dv, back_k, back_v)


def attention_kernel(parts, outs, first_head, slots_ref, reads_ref, before_ref, start_ref, order_ref, *refs):
    q_ref, do_ref, k_ref, v_ref, kt_ref, vt_ref = refs[:6]
    refs = refs[6:]
    ck_refs, cv_refs, refs = refs[:parts], refs[parts : 2 * parts], refs[2 * parts :]
    dq_ref, dk_ref, dv_ref, dkt_ref, dvt_ref = refs[:5]
    refs = refs[5:]
    gk_refs, gv_refs, refs = refs[:outs], refs[outs : 2 * outs], refs[2 * outs :]
    kx, vx, dkx, dvx = refs[:4]
    if parts > 1:
        ckx, cvx, gkx, gvx = refs[4:]
    else:
        ckx, cvx, gkx, gvx = ck_refs[0], cv_refs[0], gk_refs[0], gv_refs[0]
    rows = q_ref.shape[0]
    span = WINDOW + TILE
    chunk, chunks = pl.program_id(1), pl.num_programs(1)
    group = (first_head + pl.program_id(0)) // GROUP_HEADS
    table = (group * chunks + order_ref[chunk]) * (rows // BLOCK)

    kx[:WINDOW] = kt_ref[...]
    kx[WINDOW:] = k_ref[...]
    vx[:WINDOW] = vt_ref[...]
    vx[WINDOW:] = v_ref[...]
    dkx[...] = jnp.zeros_like(dkx)
    dvx[...] = jnp.zeros_like(dvx)

    @pl.when(chunk == 0)
    def _():
        gkx[...] = jnp.zeros_like(gkx)
        gvx[...] = jnp.zeros_like(gvx)
        if parts > 1:
            part_rows = ck_refs[0].shape[0]
            for p in range(parts):
                ckx[p * part_rows : (p + 1) * part_rows] = ck_refs[p][...]
                cvx[p * part_rows : (p + 1) * part_rows] = cv_refs[p][...]

    key_at = lax.broadcasted_iota(jnp.int32, (TILE, TILE), 0)
    query_at = lax.broadcasted_iota(jnp.int32, (TILE, TILE), 1)
    first_half = lax.broadcasted_iota(jnp.int32, (1, TILE), 1) < BLOCK
    first_rows = lax.broadcasted_iota(jnp.int32, (TILE, 1), 0) < BLOCK
    at_start = start_ref[chunk]

    def tile(t, carry):
        at = pl.multiple_of(t * TILE, TILE)
        q = q_ref[pl.ds(at, TILE)]
        do = do_ref[pl.ds(at, TILE)]
        k_loc = kx[pl.ds(at, span)]
        v_loc = vx[pl.ds(at, span)]
        places = []
        k_mem, v_mem = [], []
        for b in range(TILE // BLOCK):
            block = (table + t * (TILE // BLOCK) + b) * READS
            where = [pl.multiple_of(slots_ref[reads_ref[block + r]] * BLOCK, BLOCK) for r in range(READS)]
            places.append(where)
            k_mem.append(jnp.concatenate([ckx[pl.ds(w, BLOCK)] for w in where], 0))
            v_mem.append(jnp.concatenate([cvx[pl.ds(w, BLOCK)] for w in where], 0))

        s_loc = dot(k_loc, q, (1, 1))
        s_mem = jnp.where(first_half, dot(k_mem[0], q, (1, 1)), dot(k_mem[1], q, (1, 1)))
        pieces = []
        for c in range(span // TILE):
            piece = s_loc[c * TILE : (c + 1) * TILE]
            if c < span // TILE - 1:
                before = (at_start > 0) & (at + c * TILE < WINDOW)
                piece = piece + jnp.where(before, MASKED, 0.0)
            else:
                piece = jnp.where(key_at <= query_at, piece, MASKED)
            if c == 0:
                piece = jnp.where(key_at >= query_at, piece, MASKED)
            pieces.append(piece)
        s_loc = jnp.concatenate(pieces, 0)
        top = jnp.maximum(jnp.max(s_loc, 0, keepdims=True), jnp.max(s_mem, 0, keepdims=True))
        unit = SCALE * math.log2(math.e)
        e_loc = jnp.exp2((s_loc - top) * unit)
        e_mem = jnp.exp2((s_mem - top) * unit)
        total = jnp.sum(e_loc, 0, keepdims=True) + jnp.sum(e_mem, 0, keepdims=True)
        inverse = 1.0 / total
        p_loc = e_loc * inverse
        p_mem = e_mem * inverse
        w_loc = p_loc.astype(jnp.bfloat16)
        w_mem = p_mem.astype(jnp.bfloat16)
        dp_loc = dot(v_loc, do, (1, 1))
        dp_mem = jnp.where(first_half, dot(v_mem[0], do, (1, 1)), dot(v_mem[1], do, (1, 1)))
        delta = jnp.sum(w_loc.astype(jnp.float32) * dp_loc, 0, keepdims=True) + jnp.sum(
            w_mem.astype(jnp.float32) * dp_mem, 0, keepdims=True
        )
        ds_loc = (p_loc * (dp_loc - delta)).astype(jnp.bfloat16)
        ds_mem = (p_mem * (dp_mem - delta)).astype(jnp.bfloat16)

        dq_mem = jnp.where(first_rows, dot(ds_mem, k_mem[0], (0, 0)), dot(ds_mem, k_mem[1], (0, 0)))
        dq_ref[pl.ds(at, TILE)] = ((dot(ds_loc, k_loc, (0, 0)) + dq_mem) * SCALE).astype(dq_ref.dtype)
        dkx[pl.ds(at, span)] += dot(ds_loc, q, (1, 0))
        dvx[pl.ds(at, span)] += dot(w_loc, do, (1, 0))
        zero = jnp.zeros_like(q)
        q_two = jnp.concatenate([jnp.where(first_rows, q, zero), jnp.where(first_rows, zero, q)], 1)
        do_two = jnp.concatenate([jnp.where(first_rows, do, zero), jnp.where(first_rows, zero, do)], 1)
        read_k = (dot(ds_mem, q_two, (1, 0)) * SCALE).astype(jnp.bfloat16).astype(jnp.float32)
        read_v = dot(w_mem, do_two, (1, 0)).astype(jnp.bfloat16).astype(jnp.float32)
        for b in range(TILE // BLOCK):
            for r in range(READS):
                here = (slice(r * BLOCK, (r + 1) * BLOCK), slice(b * HEAD_DIM, (b + 1) * HEAD_DIM))
                gkx[pl.ds(places[b][r], BLOCK)] += read_k[here]
                gvx[pl.ds(places[b][r], BLOCK)] += read_v[here]
        return carry

    lax.fori_loop(0, rows // TILE, tile, 0, unroll=UNROLL)
    dkt_ref[...] = dkx[:WINDOW] * SCALE
    dvt_ref[...] = dvx[:WINDOW]
    dk_ref[...] = dkx[WINDOW:] * SCALE
    dv_ref[...] = dvx[WINDOW:]
    if parts > 1:

        @pl.when(chunk == chunks - 1)
        def _():
            out_rows = gk_refs[0].shape[0]
            for p in range(outs):
                gk_refs[p][...] = gkx[p * out_rows : (p + 1) * out_rows]
                gv_refs[p][...] = gvx[p * out_rows : (p + 1) * out_rows]


def attention(tables, tokens_in, prev, cache, cut, group_width):
    rows, width = tokens_in.shape[0], tokens_in.shape[1] // 4
    heads, first_head = width // HEAD_DIM, cut[0] // HEAD_DIM
    group_heads = group_width // HEAD_DIM
    parts, part_rows = len(cache), cache[0].shape[0]
    outs = min(2, parts)
    out_rows = parts * part_rows // outs

    def chunk_of(offset):
        return pl.BlockSpec((WINDOW, HEAD_DIM), lambda h, j, *_: (j, h + offset))

    def before(offset):
        return pl.BlockSpec((WINDOW, HEAD_DIM), lambda h, j, slots, reads, at, *_: (at[j], h + offset))

    def column(height, offset):
        return pl.BlockSpec((height, HEAD_DIM), lambda h, j, *_: (0, h + offset))

    bf16, f32 = jnp.bfloat16, jnp.float32
    shape = jax.ShapeDtypeStruct
    scratch = [pltpu.VMEM((2 * WINDOW, HEAD_DIM), kind) for kind in (bf16, bf16, f32, f32)]
    if parts > 1:
        scratch += [pltpu.VMEM((parts * part_rows, HEAD_DIM), kind) for kind in (bf16, bf16, f32, f32)]
    pairs = heads * rows * (WINDOW + TILE + 2 * READS * BLOCK)
    results = pl.pallas_call(
        functools.partial(attention_kernel, parts, outs, first_head),
        grid_spec=pltpu.PrefetchScalarGridSpec(
            num_scalar_prefetch=5,
            grid=(heads, rows // WINDOW),
            in_specs=[chunk_of(n * heads) for n in range(4)]
            + [before(0), before(heads)]
            + [column(part_rows, first_head)] * parts
            + [column(part_rows, first_head + group_heads)] * parts,
            out_specs=[chunk_of(0)] * 5 + [column(out_rows, 0)] * (2 * outs),
            scratch_shapes=scratch,
        ),
        out_shape=[shape((rows, width), bf16)]
        + [shape((rows, width), f32)] * 4
        + [shape((out_rows, width), f32)] * (2 * outs),
        compiler_params=pltpu.CompilerParams(vmem_limit_bytes=56 * 2**20),
        cost_estimate=pl.CostEstimate(
            flops=10 * pairs * HEAD_DIM, bytes_accessed=heads * part_rows * parts * 3000, transcendentals=pairs
        ),
        name="attention",
    )(*tables, *[tokens_in] * 4, prev, prev, *cache, *cache)
    return results[:5], results[5 : 5 + outs], results[5 + outs :]


def per_device(queries, keys_local, values_local, cache_keys, cache_values, block_map, retrieved, out_grad):
    chips, zs = lax.axis_size("chip"), lax.axis_size("head")
    chip, core = lax.axis_index("chip"), lax.axis_index("core")
    rows, features = queries.shape
    cache_rows = cache_keys.shape[0]
    blk_dev = cache_rows // BLOCK
    groups = retrieved.shape[1]
    shared = groups == chips and chips in (2, 4)
    split = chips if shared else 1
    head_axes = ("chip", "head") if shared else ("head",)
    peers = split * zs
    group_width = features // peers
    low = group_width - group_width // GROUP_HEADS
    cuts = ((0, low), (low, group_width))
    tokens = rows * peers
    chunks = tokens // WINDOW
    seq_parts = min(8, 2 * chips)
    numbers = jnp.arange(chunks, dtype=jnp.int32)
    bf16, f32 = jnp.bfloat16, jnp.float32

    def exchange(array):
        return lax.all_to_all(array, head_axes, split_axis=0, concat_axis=0, tiled=True)

    def to_heads(packed):
        return exchange(packed.reshape(peers, rows, packed.shape[3])).reshape(tokens, packed.shape[3])

    def to_tokens(array):
        return exchange(array.reshape(peers, rows, array.shape[1])).reshape(split, zs, rows, array.shape[1])

    def other_core(array):
        return lax.ppermute(array, "core", [(0, 1), (1, 0)])

    def other_chip(array, by):
        return lax.ppermute(array, "chip", [(i, i ^ by) for i in range(chips)]) if by else array

    everyone = ("chip", "core")
    parts = 2 * chips
    if shared:
        before, back_at = jnp.maximum(numbers - 1 + core, 0), jnp.minimum(numbers + core, chunks - 1)
        back_on = (numbers + core < chunks).astype(jnp.int32)
        start = ((2 * numbers + core) % seq_parts == 0).astype(jnp.int32)
        order = jnp.arange(chips, dtype=jnp.int32) ^ chip
        ids = jnp.stack([other_chip(retrieved, k) for k in range(chips)])
        reads = lax.dynamic_slice_in_dim(ids, chip, 1, 2)
        reads = reads.reshape(-1)
    else:
        before, back_at, back_on = numbers, numbers, numbers + 1
        start = (lax.axis_index(everyone) % seq_parts == 0).astype(jnp.int32) + numbers
        order = numbers
        reads = jnp.transpose(retrieved, (1, 0, 2)).reshape(-1)
    owner, local = block_map // blk_dev, block_map % blk_dev
    if shared:
        slots = (((owner % 2) ^ core) * chips + ((owner // 2) ^ chip)) * blk_dev + local
    else:
        slots = block_map
    before, back_at, start = (a.astype(jnp.int32) for a in (before, back_at, start))
    tables = (slots.astype(jnp.int32), reads, before, start, order.astype(jnp.int32))

    packed = pack_tokens([queries, out_grad, keys_local, values_local], split, zs, cuts)
    if shared:
        pieces = pack_cache(cache_keys, cache_values, order)
        mine = [other_chip(piece, k) for k, piece in enumerate(pieces)]
        cache = mine + [other_core(piece) for piece in mine]
    else:
        cache = [lax.all_gather(jnp.concatenate([cache_keys, cache_values], 1), everyone, tiled=True)]

    def chunks_before(keys_values):
        if shared:
            return other_core(keys_values)
        return lax.ppermute(keys_values, everyone, [(i, i + 1) for i in range(parts - 1)])

    def send_back(grads):
        if shared:
            return other_core(grads)
        return lax.ppermute(grads, everyone, [(i + 1, i) for i in range(parts - 1)])

    def run(stage, moved):
        (low, high), width = cuts[stage], cuts[stage][1] - cuts[stage][0]
        prev = chunks_before(moved[:, 2 * width :])
        (dq, dk, dv, dkt, dvt), gk, gv = attention(tables, moved, prev, cache, cuts[stage], group_width)
        back_k, back_v = send_back(dkt), send_back(dvt)
        out = finish_tokens(back_at, back_on, dq, dk, dv, back_k, back_v)
        if not shared:
            sums = [lax.psum_scatter(g[0], everyone, scatter_dimension=0, tiled=True).astype(bf16) for g in (gk, gv)]
            return out, sums
        return out, sum_cores(gk[0], gv[0], other_core(gk[1]), other_core(gv[1]), chips)

    moved_a = to_heads(packed[0])
    moved_a, second, cache, tables = after((moved_a, packed[1], cache, tables), ())
    moved_b = to_heads(second)
    out_a, sums_a = run(0, moved_a)
    out_a, moved_b = after((out_a, moved_b), ())
    out_a = to_tokens(out_a)
    out_b, sums_b = run(1, moved_b)
    if shared:
        sums_a = [other_chip(s, k) for k, s in enumerate(sums_a)]
    out_b, out_a, sums_a = after((out_b, out_a, sums_a), ())
    if shared:
        sums_b = [other_chip(s, k) for k, s in enumerate(sums_b)]
        grad_cache = place_cache([sums_a, sums_b], order.astype(jnp.int32), cuts)
    else:
        grad_cache = [jnp.concatenate([a, b], 1) for a, b in zip(sums_a, sums_b)]
    out_b = to_tokens(out_b)
    return (*unpack_tokens([out_a, out_b], cuts, 3), *grad_cache)


def solution(mesh):
    shape = mesh.shape
    fine = Mesh(mesh.devices.reshape(shape["mem"] // 2, 2, shape["head"]), ("chip", "core", "head"))
    by_token = P(("chip", "core", "head"), None)
    by_block = P(("chip", "core"), "head")
    return jax.shard_map(
        per_device,
        mesh=fine,
        in_specs=(
            by_token,
            by_token,
            by_token,
            by_block,
            by_block,
            P(),
            P(("chip", "core"), "head", None),
            by_token,
        ),
        out_specs=(by_token, by_token, by_token, by_block, by_block),
        check_vma=False,
    )
```

```python
import functools
import math

import jax
import jax.numpy as jnp
from jax import lax
from jax.experimental import pallas as pl
from jax.experimental.pallas import tpu as pltpu
from jax.sharding import Mesh
from jax.sharding import PartitionSpec as P

HEAD_DIM = 128
GROUP_HEADS = 3
BLOCK = 64
READS = 4
WINDOW = 512
TILE = 128
MASKED = -1e30
UNROLL = 4
SCALE = 1.0 / math.sqrt(HEAD_DIM)


def dot(a, b, contract):
    return lax.dot_general(a, b, ((contract[:1], contract[1:]), ((), ())), preferred_element_type=jnp.float32)


def after(values, others):
    return lax.optimization_barrier((values, others))[0]


def moved_bytes(count):
    return pl.CostEstimate(flops=0, bytes_accessed=count, transcendentals=0)


def pack_tokens(arrays, zs, plan):
    rows, features = arrays[0].shape
    count = len(arrays)

    def body(*refs):
        for out, (places, width) in zip(refs[count:], plan):
            for p, low in enumerate(places):
                for n in range(count):
                    out[p, 0, :, n * width : (n + 1) * width] = refs[n][:, low : low + width]

    return pl.pallas_call(
        body,
        grid=(zs,),
        in_specs=[pl.BlockSpec((rows, features // zs), lambda z: (0, z))] * count,
        out_specs=[pl.BlockSpec((len(p), 1, rows, count * w), lambda z: (0, z, 0, 0)) for p, w in plan],
        out_shape=[jax.ShapeDtypeStruct((len(p), zs, rows, count * w), arrays[0].dtype) for p, w in plan],
        cost_estimate=moved_bytes(4 * count * rows * features),
        name="pack_tokens",
    )(*arrays)


def unpack_tokens(moved, places, width, features, count):
    _, zs, rows, _ = moved.shape
    group = features // zs

    def body(moved_ref, *outs):
        for p, low in enumerate(places):
            for n in range(count):
                outs[n][:, low : low + width] = moved_ref[p, 0, :, n * width : (n + 1) * width]

    return pl.pallas_call(
        body,
        grid=(zs,),
        in_specs=[pl.BlockSpec((moved.shape[0], 1, rows, moved.shape[3]), lambda z: (0, z, 0, 0))],
        out_specs=[pl.BlockSpec((rows, group), lambda z: (0, z))] * count,
        out_shape=[jax.ShapeDtypeStruct((rows, features), moved.dtype)] * count,
        cost_estimate=moved_bytes(4 * count * rows * features),
        name="unpack_tokens",
    )(moved)


def add_tokens(moved, places, width, into):
    _, zs, rows, _ = moved.shape
    count = len(into)
    group = into[0].shape[1] // zs

    def body(moved_ref, *refs):
        outs, sem = refs[count : 2 * count], refs[-1]
        copies = []
        for z in range(zs):
            for p, low in enumerate(places):
                for n in range(count):
                    source = moved_ref.at[p, z, :, pl.ds(n * width, width)]
                    target = outs[n].at[:, pl.ds(z * group + low, width)]
                    copies.append(pltpu.make_async_copy(source, target, sem.at[len(copies)]))
                    copies[-1].start()
        for copy in copies:
            copy.wait()

    anywhere = pl.BlockSpec(memory_space=pl.ANY)
    return pl.pallas_call(
        body,
        in_specs=[pl.BlockSpec(memory_space=pltpu.VMEM)] + [anywhere] * count,
        out_specs=[anywhere] * count,
        out_shape=[jax.ShapeDtypeStruct(a.shape, a.dtype) for a in into],
        scratch_shapes=[pltpu.SemaphoreType.DMA((zs * len(places) * count,))],
        input_output_aliases={n + 1: n for n in range(count)},
        cost_estimate=moved_bytes(4 * count * rows * zs * len(places) * width),
        name="add_tokens",
    )(moved, *into)


def pack_cache(cache_k, cache_v, order):
    rows, features = cache_k.shape
    parts = order.shape[0]
    group = features // parts

    def body(order_ref, k_ref, v_ref, *outs):
        for p in range(parts):

            @pl.when(pl.program_id(0) == p)
            def _(p=p):
                outs[p][:, :group] = k_ref[...]
                outs[p][:, group:] = v_ref[...]

    return pl.pallas_call(
        body,
        grid_spec=pltpu.PrefetchScalarGridSpec(
            num_scalar_prefetch=1,
            grid=(parts,),
            in_specs=[pl.BlockSpec((rows, group), lambda p, order: (0, order[p]))] * 2,
            out_specs=[pl.BlockSpec((rows, 2 * group), lambda p, order: (0, 0))] * parts,
        ),
        out_shape=[jax.ShapeDtypeStruct((rows, 2 * group), cache_k.dtype)] * parts,
        compiler_params=pltpu.CompilerParams(vmem_limit_bytes=32 * 2**20),
        cost_estimate=moved_bytes(8 * rows * features),
        name="pack_cache",
    )(order, cache_k, cache_v)


def sum_cores(mine_k, mine_v, recv_k, recv_v, parts):
    rows, width = mine_k.shape[0] // parts, mine_k.shape[1]

    def body(mine_k_ref, mine_v_ref, recv_k_ref, recv_v_ref, *outs):
        for p in range(parts):

            @pl.when(pl.program_id(0) == p)
            def _(p=p):
                outs[p][:, :width] = (mine_k_ref[...] + recv_k_ref[...]).astype(outs[p].dtype)
                outs[p][:, width:] = (mine_v_ref[...] + recv_v_ref[...]).astype(outs[p].dtype)

    return pl.pallas_call(
        body,
        grid=(parts,),
        in_specs=[pl.BlockSpec((rows, width), lambda p: (p, 0))] * 4,
        out_specs=[pl.BlockSpec((rows, 2 * width), lambda p: (0, 0))] * parts,
        out_shape=[jax.ShapeDtypeStruct((rows, 2 * width), jnp.bfloat16)] * parts,
        compiler_params=pltpu.CompilerParams(vmem_limit_bytes=32 * 2**20),
        cost_estimate=moved_bytes(20 * parts * rows * width),
        name="sum_cores",
    )(mine_k, mine_v, recv_k, recv_v)


def merge_cores(first, mine_k, mine_v, recv_k, recv_v, parts):
    rows, width = mine_k.shape[0] // parts, mine_k.shape[1]

    def body(first_ref, mine_k_ref, mine_v_ref, recv_k_ref, recv_v_ref, *outs):
        mine = pl.multiple_of(first_ref[0] * width, width)
        recv = pl.multiple_of((1 - first_ref[0]) * width, width)
        for p in range(parts):

            @pl.when(pl.program_id(0) == p)
            def _(p=p):
                outs[p][:, pl.ds(mine, width)] = mine_k_ref[...]
                outs[p][:, pl.ds(recv, width)] = recv_k_ref[...]
                outs[p][:, pl.ds(mine + 2 * width, width)] = mine_v_ref[...]
                outs[p][:, pl.ds(recv + 2 * width, width)] = recv_v_ref[...]

    return pl.pallas_call(
        body,
        grid_spec=pltpu.PrefetchScalarGridSpec(
            num_scalar_prefetch=1,
            grid=(parts,),
            in_specs=[pl.BlockSpec((rows, width), lambda p, first: (p, 0))] * 4,
            out_specs=[pl.BlockSpec((rows, 4 * width), lambda p, first: (0, 0))] * parts,
        ),
        out_shape=[jax.ShapeDtypeStruct((rows, 4 * width), jnp.bfloat16)] * parts,
        compiler_params=pltpu.CompilerParams(vmem_limit_bytes=32 * 2**20),
        cost_estimate=moved_bytes(16 * parts * rows * width),
        name="merge_cores",
    )(first, mine_k, mine_v, recv_k, recv_v)


def place_cache(stages, order, cuts):
    parts = order.shape[0]
    rows, group = stages[0][0].shape[0], cuts[-1][1]
    arrays = [a for stage in stages for a in stage]

    def body(order_ref, *refs):
        k_ref, v_ref = refs[len(arrays) :]
        for p in range(parts):

            @pl.when(pl.program_id(0) == p)
            def _(p=p):
                for s, (low, high) in enumerate(cuts):
                    k_ref[:, low:high] = refs[s * parts + p][:, : high - low]
                    v_ref[:, low:high] = refs[s * parts + p][:, high - low :]

    return pl.pallas_call(
        body,
        grid_spec=pltpu.PrefetchScalarGridSpec(
            num_scalar_prefetch=1,
            grid=(parts,),
            in_specs=[pl.BlockSpec(a.shape, lambda p, order: (0, 0)) for a in arrays],
            out_specs=[pl.BlockSpec((rows, group), lambda p, order: (0, order[p]))] * 2,
        ),
        out_shape=[jax.ShapeDtypeStruct((rows, parts * group), arrays[0].dtype)] * 2,
        compiler_params=pltpu.CompilerParams(vmem_limit_bytes=32 * 2**20),
        cost_estimate=moved_bytes(8 * rows * parts * group),
        name="place_cache",
    )(order, *arrays)


def finish_tokens(back_at, back_on, dq, dk, dv, back_k, back_v):
    tokens, width = dq.shape

    def body(back_at_ref, back_on_ref, dq_ref, dk_ref, dv_ref, back_k_ref, back_v_ref, out_ref):
        on = back_on_ref[pl.program_id(0)] > 0
        out_ref[:, :width] = dq_ref[...]
        out_ref[:, width : 2 * width] = (dk_ref[...] + jnp.where(on, back_k_ref[...].astype(jnp.float32), 0.0)).astype(out_ref.dtype)
        out_ref[:, 2 * width :] = (dv_ref[...] + jnp.where(on, back_v_ref[...].astype(jnp.float32), 0.0)).astype(out_ref.dtype)

    own = pl.BlockSpec((WINDOW, width), lambda j, at, on: (j, 0))
    back = pl.BlockSpec((WINDOW, width), lambda j, at, on: (at[j], 0))
    return pl.pallas_call(
        body,
        grid_spec=pltpu.PrefetchScalarGridSpec(
            num_scalar_prefetch=2,
            grid=(tokens // WINDOW,),
            in_specs=[own, own, own, back, back],
            out_specs=pl.BlockSpec((WINDOW, 3 * width), lambda j, at, on: (j, 0)),
        ),
        out_shape=jax.ShapeDtypeStruct((tokens, 3 * width), jnp.bfloat16),
        compiler_params=pltpu.CompilerParams(vmem_limit_bytes=32 * 2**20),
        cost_estimate=moved_bytes(24 * tokens * width),
        name="finish_tokens",
    )(back_at, back_on, dq, dk, dv, back_k, back_v)


def attention_kernel(parts, outs, linked, slots_ref, reads_ref, before_ref, start_ref, order_ref, first_ref, *refs):
    q_ref, do_ref, k_ref, v_ref = refs[:4]
    refs = refs[4:]
    if not linked:
        kt_ref, vt_ref = refs[:2]
        refs = refs[2:]
    ck_refs, cv_refs, refs = refs[:parts], refs[parts : 2 * parts], refs[2 * parts :]
    if linked:
        grads_ref = refs[0]
        refs = refs[1:]
    else:
        dq_ref, dk_ref, dv_ref, dkt_ref, dvt_ref = refs[:5]
        refs = refs[5:]
    gk_refs, gv_refs, refs = refs[:outs], refs[outs : 2 * outs], refs[2 * outs :]
    kx, vx, dkx, dvx = refs[:4]
    if parts > 1:
        ckx, cvx, gkx, gvx = refs[4:]
    else:
        ckx, cvx, gkx, gvx = ck_refs[0], cv_refs[0], gk_refs[0], gv_refs[0]
    rows = q_ref.shape[0]
    span = WINDOW + TILE
    chunk, chunks = pl.program_id(1), pl.num_programs(1)
    group = (first_ref[0] + pl.program_id(0)) // GROUP_HEADS
    table = (group * chunks + order_ref[chunk]) * (rows // BLOCK)

    if linked:
        for ref in (kx, vx, dkx, dvx):
            ref[:WINDOW] = ref[WINDOW:]

        @pl.when(chunk == 0)
        def _():
            for ref in (kx, vx, dkx, dvx):
                ref[:WINDOW] = jnp.zeros((WINDOW, HEAD_DIM), ref.dtype)

        dkx[WINDOW:] = jnp.zeros((WINDOW, HEAD_DIM), jnp.float32)
        dvx[WINDOW:] = jnp.zeros((WINDOW, HEAD_DIM), jnp.float32)
    else:
        kx[:WINDOW] = kt_ref[...]
        vx[:WINDOW] = vt_ref[...]
        dkx[...] = jnp.zeros_like(dkx)
        dvx[...] = jnp.zeros_like(dvx)
    kx[WINDOW:] = k_ref[...]
    vx[WINDOW:] = v_ref[...]

    @pl.when(chunk == 0)
    def _():
        gkx[...] = jnp.zeros_like(gkx)
        gvx[...] = jnp.zeros_like(gvx)
        if parts > 1:
            part_rows = ck_refs[0].shape[0]
            for p in range(parts):
                ckx[p * part_rows : (p + 1) * part_rows] = ck_refs[p][...]
                cvx[p * part_rows : (p + 1) * part_rows] = cv_refs[p][...]

    key_at = lax.broadcasted_iota(jnp.int32, (TILE, TILE), 0)
    query_at = lax.broadcasted_iota(jnp.int32, (TILE, TILE), 1)
    first_half = lax.broadcasted_iota(jnp.int32, (1, TILE), 1) < BLOCK
    first_rows = lax.broadcasted_iota(jnp.int32, (TILE, 1), 0) < BLOCK
    at_start = start_ref[chunk]

    def tile(t, carry):
        at = pl.multiple_of(t * TILE, TILE)
        q = q_ref[pl.ds(at, TILE)]
        do = do_ref[pl.ds(at, TILE)]
        k_loc = kx[pl.ds(at, span)]
        v_loc = vx[pl.ds(at, span)]
        places = []
        k_mem, v_mem = [], []
        for b in range(TILE // BLOCK):
            block = (table + t * (TILE // BLOCK) + b) * READS
            where = [pl.multiple_of(slots_ref[reads_ref[block + r]] * BLOCK, BLOCK) for r in range(READS)]
            places.append(where)
            k_mem.append(jnp.concatenate([ckx[pl.ds(w, BLOCK)] for w in where], 0))
            v_mem.append(jnp.concatenate([cvx[pl.ds(w, BLOCK)] for w in where], 0))

        s_loc = dot(k_loc, q, (1, 1))
        s_mem = jnp.where(first_half, dot(k_mem[0], q, (1, 1)), dot(k_mem[1], q, (1, 1)))
        pieces = []
        for c in range(span // TILE):
            piece = s_loc[c * TILE : (c + 1) * TILE]
            if c < span // TILE - 1:
                before = (at_start > 0) & (at + c * TILE < WINDOW)
                piece = piece + jnp.where(before, MASKED, 0.0)
            else:
                piece = jnp.where(key_at <= query_at, piece, MASKED)
            if c == 0:
                piece = jnp.where(key_at >= query_at, piece, MASKED)
            pieces.append(piece)
        s_loc = jnp.concatenate(pieces, 0)
        top = jnp.maximum(jnp.max(s_loc, 0, keepdims=True), jnp.max(s_mem, 0, keepdims=True))
        unit = SCALE * math.log2(math.e)
        e_loc = jnp.exp2((s_loc - top) * unit)
        e_mem = jnp.exp2((s_mem - top) * unit)
        total = jnp.sum(e_loc, 0, keepdims=True) + jnp.sum(e_mem, 0, keepdims=True)
        inverse = 1.0 / total
        p_loc = e_loc * inverse
        p_mem = e_mem * inverse
        w_loc = p_loc.astype(jnp.bfloat16)
        w_mem = p_mem.astype(jnp.bfloat16)
        dp_loc = dot(v_loc, do, (1, 1))
        dp_mem = jnp.where(first_half, dot(v_mem[0], do, (1, 1)), dot(v_mem[1], do, (1, 1)))
        delta = jnp.sum(w_loc.astype(jnp.float32) * dp_loc, 0, keepdims=True) + jnp.sum(
            w_mem.astype(jnp.float32) * dp_mem, 0, keepdims=True
        )
        ds_loc = (p_loc * (dp_loc - delta)).astype(jnp.bfloat16)
        ds_mem = (p_mem * (dp_mem - delta)).astype(jnp.bfloat16)

        dq_mem = jnp.where(first_rows, dot(ds_mem, k_mem[0], (0, 0)), dot(ds_mem, k_mem[1], (0, 0)))
        dq = ((dot(ds_loc, k_loc, (0, 0)) + dq_mem) * SCALE).astype(jnp.bfloat16)
        if linked:
            grads_ref[pl.ds(pl.multiple_of(chunk * rows + at, TILE), TILE), :HEAD_DIM] = dq
        else:
            dq_ref[pl.ds(at, TILE)] = dq
        dkx[pl.ds(at, span)] += dot(ds_loc, q, (1, 0))
        dvx[pl.ds(at, span)] += dot(w_loc, do, (1, 0))
        zero = jnp.zeros_like(q)
        q_two = jnp.concatenate([jnp.where(first_rows, q, zero), jnp.where(first_rows, zero, q)], 1)
        do_two = jnp.concatenate([jnp.where(first_rows, do, zero), jnp.where(first_rows, zero, do)], 1)
        read_k = (dot(ds_mem, q_two, (1, 0)) * SCALE).astype(jnp.bfloat16).astype(jnp.float32)
        read_v = dot(w_mem, do_two, (1, 0)).astype(jnp.bfloat16).astype(jnp.float32)
        for b in range(TILE // BLOCK):
            for r in range(READS):
                here = (slice(r * BLOCK, (r + 1) * BLOCK), slice(b * HEAD_DIM, (b + 1) * HEAD_DIM))
                gkx[pl.ds(places[b][r], BLOCK)] += read_k[here]
                gvx[pl.ds(places[b][r], BLOCK)] += read_v[here]
        return carry

    lax.fori_loop(0, rows // TILE, tile, 0, unroll=UNROLL)
    if linked:

        def put(first, low):
            there = pl.ds(pl.multiple_of(first, WINDOW), WINDOW)
            here = slice(low, low + WINDOW)
            grads_ref[there, HEAD_DIM : 2 * HEAD_DIM] = (dkx[here] * SCALE).astype(grads_ref.dtype)
            grads_ref[there, 2 * HEAD_DIM :] = dvx[here].astype(grads_ref.dtype)

        @pl.when(chunk > 0)
        def _():
            put((chunk - 1) * WINDOW, 0)

        @pl.when(chunk == chunks - 1)
        def _():
            put(chunk * WINDOW, WINDOW)

    else:
        dkt_ref[...] = (dkx[:WINDOW] * SCALE).astype(dkt_ref.dtype)
        dvt_ref[...] = dvx[:WINDOW].astype(dvt_ref.dtype)
        dk_ref[...] = dkx[WINDOW:] * SCALE
        dv_ref[...] = dvx[WINDOW:]
    if parts > 1:

        @pl.when(chunk == chunks - 1)
        def _():
            out_rows = gk_refs[0].shape[0]
            for p in range(outs):
                gk_refs[p][...] = gkx[p * out_rows : (p + 1) * out_rows].astype(gk_refs[p].dtype)
                gv_refs[p][...] = gvx[p * out_rows : (p + 1) * out_rows].astype(gv_refs[p].dtype)


def attention(tables, tokens_in, prev, cache, group_width):
    rows, width = tokens_in.shape[0], tokens_in.shape[1] // 4
    heads = width // HEAD_DIM
    group_heads = group_width // HEAD_DIM
    parts, part_rows = len(cache), cache[0].shape[0]
    outs = min(2, parts)
    out_rows = parts * part_rows // outs
    linked = prev is None

    def chunk_of(offset):
        return pl.BlockSpec((WINDOW, HEAD_DIM), lambda h, j, *_: (j, h + offset))

    def before(offset):
        return pl.BlockSpec((WINDOW, HEAD_DIM), lambda h, j, slots, reads, at, *_: (at[j], h + offset))

    def column(height):
        return pl.BlockSpec((height, HEAD_DIM), lambda h, j, *_: (0, h))

    def cached(offset):
        return pl.BlockSpec((part_rows, HEAD_DIM), lambda h, j, *tables: (0, h + tables[-1][0] + offset))

    bf16, f32 = jnp.bfloat16, jnp.float32
    shape = jax.ShapeDtypeStruct
    scratch = [pltpu.VMEM((2 * WINDOW, HEAD_DIM), kind) for kind in (bf16, bf16, f32, f32)]
    if parts > 1:
        scratch += [pltpu.VMEM((parts * part_rows, HEAD_DIM), kind) for kind in (bf16, bf16, f32, f32)]
    if linked:
        token_specs = [pl.BlockSpec((rows, 3 * HEAD_DIM), lambda h, j, *_: (0, h))]
        token_shapes = [shape((rows, 3 * width), bf16)]
    else:
        token_specs = [chunk_of(0)] * 5
        token_shapes = [shape((rows, width), kind) for kind in (bf16, f32, f32, bf16, bf16)]
    pairs = heads * rows * (WINDOW + TILE + 2 * READS * BLOCK)
    results = pl.pallas_call(
        functools.partial(attention_kernel, parts, outs, linked),
        grid_spec=pltpu.PrefetchScalarGridSpec(
            num_scalar_prefetch=6,
            grid=(heads, rows // WINDOW),
            in_specs=[chunk_of(n * heads) for n in range(4)]
            + ([] if linked else [before(0), before(heads)])
            + [cached(0)] * parts
            + [cached(group_heads)] * parts,
            out_specs=token_specs + [column(out_rows)] * (2 * outs),
            scratch_shapes=scratch,
        ),
        out_shape=token_shapes + [shape((out_rows, width), bf16 if linked else f32)] * (2 * outs),
        compiler_params=pltpu.CompilerParams(vmem_limit_bytes=56 * 2**20),
        cost_estimate=pl.CostEstimate(
            flops=10 * pairs * HEAD_DIM, bytes_accessed=heads * part_rows * parts * 3000, transcendentals=pairs
        ),
        name="attention",
    )(*tables, *[tokens_in] * 4, *([] if linked else [prev, prev]), *cache, *cache)
    count = len(token_specs)
    return results[:count], results[count : count + outs], results[count + outs :]


def per_device(queries, keys_local, values_local, cache_keys, cache_values, block_map, retrieved, out_grad):
    chips, zs = lax.axis_size("chip"), lax.axis_size("head")
    chip, core = lax.axis_index("chip"), lax.axis_index("core")
    rows, features = queries.shape
    cache_rows = cache_keys.shape[0]
    blk_dev = cache_rows // BLOCK
    groups = retrieved.shape[1]
    shared = groups == chips and chips in (2, 4)
    split = chips if shared else 1
    group_width = features // (split * zs)
    low = 2 * HEAD_DIM
    cuts = ((0, low), (low, group_width))
    firsts = [g * group_width for g in range(split)]
    if shared:
        axes = (("chip", "core", "head"), ("chip", "head"))
        plan = (([g + c * HEAD_DIM for g in firsts for c in range(2)], HEAD_DIM), ([g + low for g in firsts], HEAD_DIM))
    else:
        axes = (("head",), ("head",))
        plan = tuple(([g + a for g in firsts], b - a) for a, b in cuts)
    seq_parts = min(8, 2 * chips)
    bf16 = jnp.bfloat16

    def exchange(array, stage):
        return lax.all_to_all(array, axes[stage], split_axis=0, concat_axis=0, tiled=True)

    def to_heads(packed, stage):
        places, _, _, width = packed.shape
        return exchange(packed.reshape(places * zs, rows, width), stage).reshape(places * zs * rows, width)

    def to_tokens(array, stage):
        places, width = len(plan[stage][0]), array.shape[1]
        return exchange(array.reshape(places * zs, rows, width), stage).reshape(places, zs, rows, width)

    def other_core(array):
        return lax.ppermute(array, "core", [(0, 1), (1, 0)])

    def other_chip(array, by):
        return lax.ppermute(array, "chip", [(i, i ^ by) for i in range(chips)]) if by else array

    def ints(*arrays):
        return tuple(a.astype(jnp.int32) for a in arrays)

    everyone = ("chip", "core")
    parts = 2 * chips
    owner, local = block_map // blk_dev, block_map % blk_dev
    if shared:
        chip_order = jnp.arange(chips, dtype=jnp.int32) ^ chip
        arrived = [other_chip(retrieved, k) for k in range(chips)]
        ids = lax.dynamic_slice_in_dim(jnp.stack(arrived), chip, 1, 2)
        reads = jnp.concatenate([ids.reshape(-1), other_core(ids).reshape(-1)])
        slots = (((owner % 2) ^ core) * chips + ((owner // 2) ^ chip)) * blk_dev + local
        mem = jnp.arange(parts, dtype=jnp.int32)
        start_a = (mem % seq_parts == 0) + 0 * mem
        order_a = ((mem % 2) ^ core) * chips + ((mem // 2) ^ chip)
        tables_a = ints(slots, reads, mem, start_a, order_a, core.reshape(1))
        numbers = jnp.arange(chips, dtype=jnp.int32)
        before, back_at = jnp.maximum(numbers - 1 + core, 0), jnp.minimum(numbers + core, chips - 1)
        back_on = numbers + core < chips
        start_b = (2 * numbers + core) % seq_parts == 0
        tables_b = ints(slots, reads, before, start_b, chip_order, jnp.full((1,), low // HEAD_DIM))
        backs = ints(back_at, back_on)
    else:
        arrived = []
        zero = jnp.zeros((1,), jnp.int32)
        reads = jnp.transpose(retrieved, (1, 0, 2)).reshape(-1)
        start = (lax.axis_index(everyone) % seq_parts == 0).reshape(1)
        tables_a = ints(block_map, reads, zero, start, zero, zero)
        tables_b = ints(block_map, reads, zero, start, zero, zero + low // HEAD_DIM)
        backs = (zero, zero + 1)
    tables = (tables_a, tables_b)

    packed = pack_tokens([queries, out_grad, keys_local, values_local], zs, plan)
    late = []
    if shared:
        pieces = pack_cache(cache_keys, cache_values, chip_order)
        mine = [other_chip(piece, k) for k, piece in enumerate(pieces)]
        theirs = [other_core(piece) for piece in mine]
        early, late = mine + theirs[:-1], theirs[-1:]
    else:
        early = [lax.all_gather(jnp.concatenate([cache_keys, cache_values], 1), everyone, tiled=True)]

    def chunks_before(keys_values):
        if shared:
            return other_core(keys_values)
        return lax.ppermute(keys_values, everyone, [(i, i + 1) for i in range(parts - 1)])

    def send_back(grads):
        if shared:
            return other_core(grads)
        return lax.ppermute(grads, everyone, [(i + 1, i) for i in range(parts - 1)])

    def by_tokens(stage, moved):
        width = moved.shape[1] // 4
        prev = chunks_before(moved[:, 2 * width :])
        (dq, dk, dv, dkt, dvt), gk, gv = attention(tables[stage], moved, prev, cache, group_width)
        out = finish_tokens(*backs, dq, dk, dv, send_back(dkt), send_back(dvt))
        if not shared:
            return out, [lax.psum_scatter(g[0], everyone, scatter_dimension=0, tiled=True).astype(bf16) for g in (gk, gv)]
        return out, sum_cores(gk[0], gv[0], other_core(gk[1]), other_core(gv[1]), chips)

    def by_heads(stage, moved):
        (out,), gk, gv = attention(tables[stage], moved, None, cache, group_width)
        return out, (gk, gv)

    moved_a = to_heads(after(packed[0], arrived), 0)
    moved_a, second, early, tables = after((moved_a, packed[1], early, tables), ())
    cache = early + late
    moved_b = to_heads(second, 1)
    out_a, sums_a = (by_heads if shared else by_tokens)(0, moved_a)
    out_a, moved_b = after((out_a, moved_b), ())
    out_a = to_tokens(out_a, 0)
    out_b, sums_b = by_tokens(1, moved_b)
    if shared:
        gk, gv = sums_a
        sums_a = merge_cores(tables_a[5], gk[0], gv[0], other_core(gk[1]), other_core(gv[1]), chips)
        sums_a = [other_chip(s, k) for k, s in enumerate(sums_a)]
    out_b, out_a, sums_a, sums_b = after((out_b, out_a, sums_a, sums_b), ())
    if shared:
        sums_b = [other_chip(s, k) for k, s in enumerate(sums_b)]
        grad_cache = place_cache([sums_a, sums_b], chip_order, cuts)
    else:
        grad_cache = [jnp.concatenate([a, b], 1) for a, b in zip(sums_a, sums_b)]
    grads = unpack_tokens(out_a, *plan[0], features, 3)
    out_b = to_tokens(out_b, 1)
    return (*add_tokens(out_b, *plan[1], grads), *grad_cache)


def solution(mesh):
    shape = mesh.shape
    fine = Mesh(mesh.devices.reshape(shape["mem"] // 2, 2, shape["head"]), ("chip", "core", "head"))
    by_token = P(("chip", "core", "head"), None)
    by_block = P(("chip", "core"), "head")
    return jax.shard_map(
        per_device,
        mesh=fine,
        in_specs=(
            by_token,
            by_token,
            by_token,
            by_block,
            by_block,
            P(),
            P(("chip", "core"), "head", None),
            by_token,
        ),
        out_specs=(by_token, by_token, by_token, by_block, by_block),
        check_vma=False,
    )
```

```python
import functools
import math

import jax
import jax.numpy as jnp
from jax import lax
from jax.experimental import pallas as pl
from jax.experimental.pallas import tpu as pltpu
from jax.sharding import Mesh
from jax.sharding import PartitionSpec as P

HEAD_DIM = 128
GROUP_HEADS = 3
BLOCK = 64
READS = 4
WINDOW = 512
TILE = 128
MASKED = -1e30
UNROLL = 4
SCALE = 1.0 / math.sqrt(HEAD_DIM)


def dot(a, b, contract):
    return lax.dot_general(a, b, ((contract[:1], contract[1:]), ((), ())), preferred_element_type=jnp.float32)


def after(values, others):
    return lax.optimization_barrier((values, others))[0]


def moved_bytes(count):
    return pl.CostEstimate(flops=0, bytes_accessed=count, transcendentals=0)


def pack_tokens(arrays, zs, plan):
    rows, features = arrays[0].shape
    count = len(arrays)

    def body(*refs):
        for out, (places, width) in zip(refs[count:], plan):
            for p, low in enumerate(places):
                for n in range(count):
                    out[p, 0, :, n * width : (n + 1) * width] = refs[n][:, low : low + width]

    return pl.pallas_call(
        body,
        grid=(zs,),
        in_specs=[pl.BlockSpec((rows, features // zs), lambda z: (0, z))] * count,
        out_specs=[pl.BlockSpec((len(p), 1, rows, count * w), lambda z: (0, z, 0, 0)) for p, w in plan],
        out_shape=[jax.ShapeDtypeStruct((len(p), zs, rows, count * w), arrays[0].dtype) for p, w in plan],
        cost_estimate=moved_bytes(4 * count * rows * features),
        name="pack_tokens",
    )(*arrays)


def unpack_tokens(moved, places, width, features, count):
    _, zs, rows, _ = moved.shape
    group = features // zs

    def body(moved_ref, *outs):
        for p, low in enumerate(places):
            for n in range(count):
                outs[n][:, low : low + width] = moved_ref[p, 0, :, n * width : (n + 1) * width]

    return pl.pallas_call(
        body,
        grid=(zs,),
        in_specs=[pl.BlockSpec((moved.shape[0], 1, rows, moved.shape[3]), lambda z: (0, z, 0, 0))],
        out_specs=[pl.BlockSpec((rows, group), lambda z: (0, z))] * count,
        out_shape=[jax.ShapeDtypeStruct((rows, features), moved.dtype)] * count,
        cost_estimate=moved_bytes(4 * count * rows * features),
        name="unpack_tokens",
    )(moved)


def add_tokens(moved, places, width, into):
    _, zs, rows, _ = moved.shape
    count = len(into)
    group = into[0].shape[1] // zs

    def body(moved_ref, *refs):
        outs, sem = refs[count : 2 * count], refs[-1]
        copies = []
        for z in range(zs):
            for p, low in enumerate(places):
                for n in range(count):
                    source = moved_ref.at[p, z, :, pl.ds(n * width, width)]
                    target = outs[n].at[:, pl.ds(z * group + low, width)]
                    copies.append(pltpu.make_async_copy(source, target, sem.at[len(copies)]))
                    copies[-1].start()
        for copy in copies:
            copy.wait()

    anywhere = pl.BlockSpec(memory_space=pl.ANY)
    return pl.pallas_call(
        body,
        in_specs=[pl.BlockSpec(memory_space=pltpu.VMEM)] + [anywhere] * count,
        out_specs=[anywhere] * count,
        out_shape=[jax.ShapeDtypeStruct(a.shape, a.dtype) for a in into],
        scratch_shapes=[pltpu.SemaphoreType.DMA((zs * len(places) * count,))],
        input_output_aliases={n + 1: n for n in range(count)},
        cost_estimate=moved_bytes(4 * count * rows * zs * len(places) * width),
        name="add_tokens",
    )(moved, *into)


def pack_cache(cache_k, cache_v, order, cuts):
    rows, features = cache_k.shape
    parts = order.shape[0]
    group = features // parts

    def body(order_ref, k_ref, v_ref, *outs):
        for p in range(parts):

            @pl.when(pl.program_id(0) == p)
            def _(p=p):
                for s, (low, high) in enumerate(cuts):
                    outs[s * parts + p][:, : high - low] = k_ref[:, low:high]
                    outs[s * parts + p][:, high - low :] = v_ref[:, low:high]

    widths = [2 * (high - low) for low, high in cuts for _ in range(parts)]
    outs = pl.pallas_call(
        body,
        grid_spec=pltpu.PrefetchScalarGridSpec(
            num_scalar_prefetch=1,
            grid=(parts,),
            in_specs=[pl.BlockSpec((rows, group), lambda p, order: (0, order[p]))] * 2,
            out_specs=[pl.BlockSpec((rows, w), lambda p, order: (0, 0)) for w in widths],
        ),
        out_shape=[jax.ShapeDtypeStruct((rows, w), cache_k.dtype) for w in widths],
        compiler_params=pltpu.CompilerParams(vmem_limit_bytes=32 * 2**20),
        cost_estimate=moved_bytes(8 * rows * features),
        name="pack_cache",
    )(order, cache_k, cache_v)
    return [outs[s * parts : (s + 1) * parts] for s in range(len(cuts))]


def sum_cores(mine_k, mine_v, recv_k, recv_v, parts):
    rows, width = mine_k.shape[0] // parts, mine_k.shape[1]

    def body(mine_k_ref, mine_v_ref, recv_k_ref, recv_v_ref, *outs):
        for p in range(parts):

            @pl.when(pl.program_id(0) == p)
            def _(p=p):
                outs[p][:, :width] = (mine_k_ref[...] + recv_k_ref[...]).astype(outs[p].dtype)
                outs[p][:, width:] = (mine_v_ref[...] + recv_v_ref[...]).astype(outs[p].dtype)

    return pl.pallas_call(
        body,
        grid=(parts,),
        in_specs=[pl.BlockSpec((rows, width), lambda p: (p, 0))] * 4,
        out_specs=[pl.BlockSpec((rows, 2 * width), lambda p: (0, 0))] * parts,
        out_shape=[jax.ShapeDtypeStruct((rows, 2 * width), jnp.bfloat16)] * parts,
        compiler_params=pltpu.CompilerParams(vmem_limit_bytes=32 * 2**20),
        cost_estimate=moved_bytes(20 * parts * rows * width),
        name="sum_cores",
    )(mine_k, mine_v, recv_k, recv_v)


def merge_cores(first, mine_k, mine_v, recv_k, recv_v, parts):
    rows, width = mine_k.shape[0] // parts, mine_k.shape[1]

    def body(first_ref, mine_k_ref, mine_v_ref, recv_k_ref, recv_v_ref, *outs):
        mine = pl.multiple_of(first_ref[0] * width, width)
        recv = pl.multiple_of((1 - first_ref[0]) * width, width)
        for p in range(parts):

            @pl.when(pl.program_id(0) == p)
            def _(p=p):
                outs[p][:, pl.ds(mine, width)] = mine_k_ref[...]
                outs[p][:, pl.ds(recv, width)] = recv_k_ref[...]
                outs[p][:, pl.ds(mine + 2 * width, width)] = mine_v_ref[...]
                outs[p][:, pl.ds(recv + 2 * width, width)] = recv_v_ref[...]

    return pl.pallas_call(
        body,
        grid_spec=pltpu.PrefetchScalarGridSpec(
            num_scalar_prefetch=1,
            grid=(parts,),
            in_specs=[pl.BlockSpec((rows, width), lambda p, first: (p, 0))] * 4,
            out_specs=[pl.BlockSpec((rows, 4 * width), lambda p, first: (0, 0))] * parts,
        ),
        out_shape=[jax.ShapeDtypeStruct((rows, 4 * width), jnp.bfloat16)] * parts,
        compiler_params=pltpu.CompilerParams(vmem_limit_bytes=32 * 2**20),
        cost_estimate=moved_bytes(16 * parts * rows * width),
        name="merge_cores",
    )(first, mine_k, mine_v, recv_k, recv_v)


def place_cache(stages, order, cuts):
    parts = order.shape[0]
    rows, group = stages[0][0].shape[0], cuts[-1][1]
    arrays = [a for stage in stages for a in stage]

    def body(order_ref, *refs):
        k_ref, v_ref = refs[len(arrays) :]
        for p in range(parts):

            @pl.when(pl.program_id(0) == p)
            def _(p=p):
                for s, (low, high) in enumerate(cuts):
                    k_ref[:, low:high] = refs[s * parts + p][:, : high - low]
                    v_ref[:, low:high] = refs[s * parts + p][:, high - low :]

    return pl.pallas_call(
        body,
        grid_spec=pltpu.PrefetchScalarGridSpec(
            num_scalar_prefetch=1,
            grid=(parts,),
            in_specs=[pl.BlockSpec(a.shape, lambda p, order: (0, 0)) for a in arrays],
            out_specs=[pl.BlockSpec((rows, group), lambda p, order: (0, order[p]))] * 2,
        ),
        out_shape=[jax.ShapeDtypeStruct((rows, parts * group), arrays[0].dtype)] * 2,
        compiler_params=pltpu.CompilerParams(vmem_limit_bytes=32 * 2**20),
        cost_estimate=moved_bytes(8 * rows * parts * group),
        name="place_cache",
    )(order, *arrays)


def finish_tokens(back_at, back_on, dq, dk, dv, back_k, back_v):
    tokens, width = dq.shape

    def body(back_at_ref, back_on_ref, dq_ref, dk_ref, dv_ref, back_k_ref, back_v_ref, out_ref):
        on = back_on_ref[pl.program_id(0)] > 0
        out_ref[:, :width] = dq_ref[...]
        out_ref[:, width : 2 * width] = (dk_ref[...] + jnp.where(on, back_k_ref[...].astype(jnp.float32), 0.0)).astype(out_ref.dtype)
        out_ref[:, 2 * width :] = (dv_ref[...] + jnp.where(on, back_v_ref[...].astype(jnp.float32), 0.0)).astype(out_ref.dtype)

    own = pl.BlockSpec((WINDOW, width), lambda j, at, on: (j, 0))
    back = pl.BlockSpec((WINDOW, width), lambda j, at, on: (at[j], 0))
    return pl.pallas_call(
        body,
        grid_spec=pltpu.PrefetchScalarGridSpec(
            num_scalar_prefetch=2,
            grid=(tokens // WINDOW,),
            in_specs=[own, own, own, back, back],
            out_specs=pl.BlockSpec((WINDOW, 3 * width), lambda j, at, on: (j, 0)),
        ),
        out_shape=jax.ShapeDtypeStruct((tokens, 3 * width), jnp.bfloat16),
        compiler_params=pltpu.CompilerParams(vmem_limit_bytes=32 * 2**20),
        cost_estimate=moved_bytes(24 * tokens * width),
        name="finish_tokens",
    )(back_at, back_on, dq, dk, dv, back_k, back_v)


def attention_kernel(parts, outs, linked, slots_ref, reads_ref, before_ref, start_ref, order_ref, first_ref, *refs):
    q_ref, do_ref, k_ref, v_ref = refs[:4]
    refs = refs[4:]
    if not linked:
        kt_ref, vt_ref = refs[:2]
        refs = refs[2:]
    ck_refs, cv_refs, refs = refs[:parts], refs[parts : 2 * parts], refs[2 * parts :]
    if linked:
        grads_ref = refs[0]
        refs = refs[1:]
    else:
        dq_ref, dk_ref, dv_ref, dkt_ref, dvt_ref = refs[:5]
        refs = refs[5:]
    gk_refs, gv_refs, refs = refs[:outs], refs[outs : 2 * outs], refs[2 * outs :]
    kx, vx, dkx, dvx = refs[:4]
    if parts > 1:
        ckx, cvx, gkx, gvx = refs[4:]
    else:
        ckx, cvx, gkx, gvx = ck_refs[0], cv_refs[0], gk_refs[0], gv_refs[0]
    rows = q_ref.shape[0]
    span = WINDOW + TILE
    chunk, chunks = pl.program_id(1), pl.num_programs(1)
    group = (first_ref[0] + pl.program_id(0)) // GROUP_HEADS
    table = (group * chunks + order_ref[chunk]) * (rows // BLOCK)

    if linked:
        for ref in (kx, vx, dkx, dvx):
            ref[:WINDOW] = ref[WINDOW:]

        @pl.when(chunk == 0)
        def _():
            for ref in (kx, vx, dkx, dvx):
                ref[:WINDOW] = jnp.zeros((WINDOW, HEAD_DIM), ref.dtype)

        dkx[WINDOW:] = jnp.zeros((WINDOW, HEAD_DIM), jnp.float32)
        dvx[WINDOW:] = jnp.zeros((WINDOW, HEAD_DIM), jnp.float32)
    else:
        kx[:WINDOW] = kt_ref[...]
        vx[:WINDOW] = vt_ref[...]
        dkx[...] = jnp.zeros_like(dkx)
        dvx[...] = jnp.zeros_like(dvx)
    kx[WINDOW:] = k_ref[...]
    vx[WINDOW:] = v_ref[...]

    @pl.when(chunk == 0)
    def _():
        gkx[...] = jnp.zeros_like(gkx)
        gvx[...] = jnp.zeros_like(gvx)
        if parts > 1:
            part_rows = ck_refs[0].shape[0]
            for p in range(parts):
                ckx[p * part_rows : (p + 1) * part_rows] = ck_refs[p][...]
                cvx[p * part_rows : (p + 1) * part_rows] = cv_refs[p][...]

    key_at = lax.broadcasted_iota(jnp.int32, (TILE, TILE), 0)
    query_at = lax.broadcasted_iota(jnp.int32, (TILE, TILE), 1)
    first_half = lax.broadcasted_iota(jnp.int32, (1, TILE), 1) < BLOCK
    first_rows = lax.broadcasted_iota(jnp.int32, (TILE, 1), 0) < BLOCK
    at_start = start_ref[chunk]

    def tile(t, carry):
        at = pl.multiple_of(t * TILE, TILE)
        q = q_ref[pl.ds(at, TILE)]
        do = do_ref[pl.ds(at, TILE)]
        k_loc = kx[pl.ds(at, span)]
        v_loc = vx[pl.ds(at, span)]
        places = []
        k_mem, v_mem = [], []
        for b in range(TILE // BLOCK):
            block = (table + t * (TILE // BLOCK) + b) * READS
            where = [pl.multiple_of(slots_ref[reads_ref[block + r]] * BLOCK, BLOCK) for r in range(READS)]
            places.append(where)
            k_mem.append(jnp.concatenate([ckx[pl.ds(w, BLOCK)] for w in where], 0))
            v_mem.append(jnp.concatenate([cvx[pl.ds(w, BLOCK)] for w in where], 0))

        s_loc = dot(k_loc, q, (1, 1))
        s_mem = jnp.where(first_half, dot(k_mem[0], q, (1, 1)), dot(k_mem[1], q, (1, 1)))
        pieces = []
        for c in range(span // TILE):
            piece = s_loc[c * TILE : (c + 1) * TILE]
            if c < span // TILE - 1:
                before = (at_start > 0) & (at + c * TILE < WINDOW)
                piece = piece + jnp.where(before, MASKED, 0.0)
            else:
                piece = jnp.where(key_at <= query_at, piece, MASKED)
            if c == 0:
                piece = jnp.where(key_at >= query_at, piece, MASKED)
            pieces.append(piece)
        s_loc = jnp.concatenate(pieces, 0)
        top = jnp.maximum(jnp.max(s_loc, 0, keepdims=True), jnp.max(s_mem, 0, keepdims=True))
        unit = SCALE * math.log2(math.e)
        e_loc = jnp.exp2((s_loc - top) * unit)
        e_mem = jnp.exp2((s_mem - top) * unit)
        total = jnp.sum(e_loc, 0, keepdims=True) + jnp.sum(e_mem, 0, keepdims=True)
        inverse = 1.0 / total
        p_loc = e_loc * inverse
        p_mem = e_mem * inverse
        w_loc = p_loc.astype(jnp.bfloat16)
        w_mem = p_mem.astype(jnp.bfloat16)
        dp_loc = dot(v_loc, do, (1, 1))
        dp_mem = jnp.where(first_half, dot(v_mem[0], do, (1, 1)), dot(v_mem[1], do, (1, 1)))
        delta = jnp.sum(w_loc.astype(jnp.float32) * dp_loc, 0, keepdims=True) + jnp.sum(
            w_mem.astype(jnp.float32) * dp_mem, 0, keepdims=True
        )
        ds_loc = (p_loc * (dp_loc - delta)).astype(jnp.bfloat16)
        ds_mem = (p_mem * (dp_mem - delta)).astype(jnp.bfloat16)

        dq_mem = jnp.where(first_rows, dot(ds_mem, k_mem[0], (0, 0)), dot(ds_mem, k_mem[1], (0, 0)))
        dq = ((dot(ds_loc, k_loc, (0, 0)) + dq_mem) * SCALE).astype(jnp.bfloat16)
        if linked:
            grads_ref[pl.ds(pl.multiple_of(chunk * rows + at, TILE), TILE), :HEAD_DIM] = dq
        else:
            dq_ref[pl.ds(at, TILE)] = dq
        dkx[pl.ds(at, span)] += dot(ds_loc, q, (1, 0))
        dvx[pl.ds(at, span)] += dot(w_loc, do, (1, 0))
        zero = jnp.zeros_like(q)
        q_two = jnp.concatenate([jnp.where(first_rows, q, zero), jnp.where(first_rows, zero, q)], 1)
        do_two = jnp.concatenate([jnp.where(first_rows, do, zero), jnp.where(first_rows, zero, do)], 1)
        read_k = (dot(ds_mem, q_two, (1, 0)) * SCALE).astype(jnp.bfloat16).astype(jnp.float32)
        read_v = dot(w_mem, do_two, (1, 0)).astype(jnp.bfloat16).astype(jnp.float32)
        for b in range(TILE // BLOCK):
            for r in range(READS):
                here = (slice(r * BLOCK, (r + 1) * BLOCK), slice(b * HEAD_DIM, (b + 1) * HEAD_DIM))
                gkx[pl.ds(places[b][r], BLOCK)] += read_k[here]
                gvx[pl.ds(places[b][r], BLOCK)] += read_v[here]
        return carry

    lax.fori_loop(0, rows // TILE, tile, 0, unroll=UNROLL)
    if linked:

        def put(first, low):
            there = pl.ds(pl.multiple_of(first, WINDOW), WINDOW)
            here = slice(low, low + WINDOW)
            grads_ref[there, HEAD_DIM : 2 * HEAD_DIM] = (dkx[here] * SCALE).astype(grads_ref.dtype)
            grads_ref[there, 2 * HEAD_DIM :] = dvx[here].astype(grads_ref.dtype)

        @pl.when(chunk > 0)
        def _():
            put((chunk - 1) * WINDOW, 0)

        @pl.when(chunk == chunks - 1)
        def _():
            put(chunk * WINDOW, WINDOW)

    else:
        dkt_ref[...] = (dkx[:WINDOW] * SCALE).astype(dkt_ref.dtype)
        dvt_ref[...] = dvx[:WINDOW].astype(dvt_ref.dtype)
        dk_ref[...] = dkx[WINDOW:] * SCALE
        dv_ref[...] = dvx[WINDOW:]
    if parts > 1:

        @pl.when(chunk == chunks - 1)
        def _():
            out_rows = gk_refs[0].shape[0]
            for p in range(outs):
                gk_refs[p][...] = gkx[p * out_rows : (p + 1) * out_rows].astype(gk_refs[p].dtype)
                gv_refs[p][...] = gvx[p * out_rows : (p + 1) * out_rows].astype(gv_refs[p].dtype)


def attention(tables, tokens_in, prev, cache):
    rows, width = tokens_in.shape[0], tokens_in.shape[1] // 4
    heads = width // HEAD_DIM
    cache_heads = cache[0].shape[1] // (2 * HEAD_DIM)
    parts, part_rows = len(cache), cache[0].shape[0]
    outs = min(2, parts)
    out_rows = parts * part_rows // outs
    linked = prev is None

    def chunk_of(offset):
        return pl.BlockSpec((WINDOW, HEAD_DIM), lambda h, j, *_: (j, h + offset))

    def before(offset):
        return pl.BlockSpec((WINDOW, HEAD_DIM), lambda h, j, slots, reads, at, *_: (at[j], h + offset))

    def column(height):
        return pl.BlockSpec((height, HEAD_DIM), lambda h, j, *_: (0, h))

    def cached(offset):
        return pl.BlockSpec((part_rows, HEAD_DIM), lambda h, j, *tables: (0, h + tables[-1][0] + offset))

    bf16, f32 = jnp.bfloat16, jnp.float32
    shape = jax.ShapeDtypeStruct
    scratch = [pltpu.VMEM((2 * WINDOW, HEAD_DIM), kind) for kind in (bf16, bf16, f32, f32)]
    if parts > 1:
        scratch += [pltpu.VMEM((parts * part_rows, HEAD_DIM), kind) for kind in (bf16, bf16, f32, f32)]
    if linked:
        token_specs = [pl.BlockSpec((rows, 3 * HEAD_DIM), lambda h, j, *_: (0, h))]
        token_shapes = [shape((rows, 3 * width), bf16)]
    else:
        token_specs = [chunk_of(0)] * 5
        token_shapes = [shape((rows, width), kind) for kind in (bf16, f32, f32, bf16, bf16)]
    pairs = heads * rows * (WINDOW + TILE + 2 * READS * BLOCK)
    results = pl.pallas_call(
        functools.partial(attention_kernel, parts, outs, linked),
        grid_spec=pltpu.PrefetchScalarGridSpec(
            num_scalar_prefetch=6,
            grid=(heads, rows // WINDOW),
            in_specs=[chunk_of(n * heads) for n in range(4)]
            + ([] if linked else [before(0), before(heads)])
            + [cached(0)] * parts
            + [cached(cache_heads)] * parts,
            out_specs=token_specs + [column(out_rows)] * (2 * outs),
            scratch_shapes=scratch,
        ),
        out_shape=token_shapes + [shape((out_rows, width), bf16 if linked else f32)] * (2 * outs),
        compiler_params=pltpu.CompilerParams(vmem_limit_bytes=56 * 2**20),
        cost_estimate=pl.CostEstimate(
            flops=10 * pairs * HEAD_DIM, bytes_accessed=heads * part_rows * parts * 3000, transcendentals=pairs
        ),
        name="attention",
    )(*tables, *[tokens_in] * 4, *([] if linked else [prev, prev]), *cache, *cache)
    count = len(token_specs)
    return results[:count], results[count : count + outs], results[count + outs :]


def per_device(queries, keys_local, values_local, cache_keys, cache_values, block_map, retrieved, out_grad):
    chips, zs = lax.axis_size("chip"), lax.axis_size("head")
    chip, core = lax.axis_index("chip"), lax.axis_index("core")
    rows, features = queries.shape
    cache_rows = cache_keys.shape[0]
    blk_dev = cache_rows // BLOCK
    groups = retrieved.shape[1]
    shared = groups == chips and chips in (2, 4)
    split = chips if shared else 1
    group_width = features // (split * zs)
    low = 2 * HEAD_DIM
    cuts = ((0, low), (low, group_width))
    firsts = [g * group_width for g in range(split)]
    if shared:
        axes = (("chip", "core", "head"), ("chip", "head"))
        plan = (([g + c * HEAD_DIM for g in firsts for c in range(2)], HEAD_DIM), ([g + low for g in firsts], HEAD_DIM))
    else:
        axes = (("head",), ("head",))
        plan = tuple(([g + a for g in firsts], b - a) for a, b in cuts)
    seq_parts = min(8, 2 * chips)
    bf16 = jnp.bfloat16

    def exchange(array, stage):
        return lax.all_to_all(array, axes[stage], split_axis=0, concat_axis=0, tiled=True)

    def to_heads(packed, stage):
        places, _, _, width = packed.shape
        return exchange(packed.reshape(places * zs, rows, width), stage).reshape(places * zs * rows, width)

    def to_tokens(array, stage):
        places, width = len(plan[stage][0]), array.shape[1]
        return exchange(array.reshape(places * zs, rows, width), stage).reshape(places, zs, rows, width)

    def other_core(array):
        return lax.ppermute(array, "core", [(0, 1), (1, 0)])

    def other_chip(array, by):
        return lax.ppermute(array, "chip", [(i, i ^ by) for i in range(chips)]) if by else array

    def ints(*arrays):
        return tuple(a.astype(jnp.int32) for a in arrays)

    everyone = ("chip", "core")
    parts = 2 * chips
    owner, local = block_map // blk_dev, block_map % blk_dev
    if shared:
        chip_order = jnp.arange(chips, dtype=jnp.int32) ^ chip
        arrived = [other_chip(retrieved, k) for k in range(chips)]
        ids = lax.dynamic_slice_in_dim(jnp.stack(arrived), chip, 1, 2)
        reads = jnp.concatenate([ids.reshape(-1), other_core(ids).reshape(-1)])
        slots = (((owner % 2) ^ core) * chips + ((owner // 2) ^ chip)) * blk_dev + local
        mem = jnp.arange(parts, dtype=jnp.int32)
        start_a = (mem % seq_parts == 0) + 0 * mem
        order_a = ((mem % 2) ^ core) * chips + ((mem // 2) ^ chip)
        tables_a = ints(slots, reads, mem, start_a, order_a, core.reshape(1))
        numbers = jnp.arange(chips, dtype=jnp.int32)
        before, back_at = jnp.maximum(numbers - 1 + core, 0), jnp.minimum(numbers + core, chips - 1)
        back_on = numbers + core < chips
        start_b = (2 * numbers + core) % seq_parts == 0
        tables_b = ints(slots, reads, before, start_b, chip_order, jnp.zeros((1,)))
        backs = ints(back_at, back_on)
    else:
        zero = jnp.zeros((1,), jnp.int32)
        reads = jnp.transpose(retrieved, (1, 0, 2)).reshape(-1)
        start = (lax.axis_index(everyone) % seq_parts == 0).reshape(1)
        tables_a = ints(block_map, reads, zero, start, zero, zero)
        tables_b = ints(block_map, reads, zero, start, zero, zero + low // HEAD_DIM)
        backs = (zero, zero + 1)
    tables = (tables_a, tables_b)

    token_arrays = [queries, out_grad, keys_local, values_local]
    (packed_a,), (packed_b,) = (pack_tokens(token_arrays, zs, [stage]) for stage in plan)
    if shared:
        pieces = pack_cache(cache_keys, cache_values, chip_order, cuts)
    else:
        cache_a = cache_b = [lax.all_gather(jnp.concatenate([cache_keys, cache_values], 1), everyone, tiled=True)]

    def spread(pieces):
        mine = [other_chip(piece, k) for k, piece in enumerate(pieces)]
        return mine + [other_core(piece) for piece in mine], mine

    def chunks_before(keys_values):
        if shared:
            return other_core(keys_values)
        return lax.ppermute(keys_values, everyone, [(i, i + 1) for i in range(parts - 1)])

    def send_back(grads):
        if shared:
            return other_core(grads)
        return lax.ppermute(grads, everyone, [(i + 1, i) for i in range(parts - 1)])

    def by_tokens(stage, moved, cache):
        width = moved.shape[1] // 4
        prev = chunks_before(moved[:, 2 * width :])
        (dq, dk, dv, dkt, dvt), gk, gv = attention(tables[stage], moved, prev, cache)
        out = finish_tokens(*backs, dq, dk, dv, send_back(dkt), send_back(dvt))
        if not shared:
            return out, [lax.psum_scatter(g[0], everyone, scatter_dimension=0, tiled=True).astype(bf16) for g in (gk, gv)]
        return out, sum_cores(gk[0], gv[0], other_core(gk[1]), other_core(gv[1]), chips)

    def by_heads(stage, moved, cache):
        (out,), gk, gv = attention(tables[stage], moved, None, cache)
        return out, (gk, gv)

    moved_b = to_heads(packed_b, 1)
    early = ()
    if shared:
        cache_b, mine = spread(pieces[1])
        early = (mine, arrived)
    moved_b, packed_a, early = after((moved_b, packed_a, early), ())
    if shared:
        cache_a, _ = spread(after(pieces[0], moved_b))
    moved_a = to_heads(packed_a, 0)
    out_b, sums_b = by_tokens(1, moved_b, cache_b)
    moved_a, out_b, sums_b, tables, cache_a = after((moved_a, out_b, sums_b, tables, cache_a), ())
    out_b = to_tokens(out_b, 1)
    out_a, sums_a = (by_heads if shared else by_tokens)(0, moved_a, cache_a)
    if shared:
        sums_b = [other_chip(s, k) for k, s in enumerate(sums_b)]
    out_a, out_b, sums_b = after((out_a, out_b, sums_b), ())
    if shared:
        gk, gv = sums_a
        sums_a = merge_cores(tables_a[5], gk[0], gv[0], other_core(gk[1]), other_core(gv[1]), chips)
        sums_a = [other_chip(s, k) for k, s in enumerate(sums_a)]
        grad_cache = place_cache([sums_a, sums_b], chip_order, cuts)
    else:
        grad_cache = [jnp.concatenate([a, b], 1) for a, b in zip(sums_a, sums_b)]
    grads = unpack_tokens(out_b, *plan[1], features, 3)
    out_a = to_tokens(out_a, 0)
    return (*add_tokens(out_a, *plan[0], grads), *grad_cache)


def solution(mesh):
    shape = mesh.shape
    fine = Mesh(mesh.devices.reshape(shape["mem"] // 2, 2, shape["head"]), ("chip", "core", "head"))
    by_token = P(("chip", "core", "head"), None)
    by_block = P(("chip", "core"), "head")
    return jax.shard_map(
        per_device,
        mesh=fine,
        in_specs=(
            by_token,
            by_token,
            by_token,
            by_block,
            by_block,
            P(),
            P(("chip", "core"), "head", None),
            by_token,
        ),
        out_specs=(by_token, by_token, by_token, by_block, by_block),
        check_vma=False,
    )
```

```python
import functools
import math

import jax
import jax.numpy as jnp
from jax import lax
from jax.experimental import pallas as pl
from jax.experimental.pallas import tpu as pltpu
from jax.sharding import Mesh
from jax.sharding import PartitionSpec as P

HEAD_DIM = 128
GROUP_HEADS = 3
BLOCK = 64
READS = 4
WINDOW = 512
TILE = 128
MASKED = -1e30
UNROLL = 4
SCALE = 1.0 / math.sqrt(HEAD_DIM)


def dot(a, b, contract):
    return lax.dot_general(a, b, ((contract[:1], contract[1:]), ((), ())), preferred_element_type=jnp.float32)


def after(values, others):
    return lax.optimization_barrier((values, others))[0]


def moved_bytes(count):
    return pl.CostEstimate(flops=0, bytes_accessed=count, transcendentals=0)


def pack_tokens(arrays, zs, plan):
    rows, features = arrays[0].shape
    count = len(arrays)

    def body(*refs):
        for out, (places, width) in zip(refs[count:], plan):
            for p, low in enumerate(places):
                for n in range(count):
                    out[p, 0, :, n * width : (n + 1) * width] = refs[n][:, low : low + width]

    return pl.pallas_call(
        body,
        grid=(zs,),
        in_specs=[pl.BlockSpec((rows, features // zs), lambda z: (0, z))] * count,
        out_specs=[pl.BlockSpec((len(p), 1, rows, count * w), lambda z: (0, z, 0, 0)) for p, w in plan],
        out_shape=[jax.ShapeDtypeStruct((len(p), zs, rows, count * w), arrays[0].dtype) for p, w in plan],
        cost_estimate=moved_bytes(4 * count * rows * features),
        name="pack_tokens",
    )(*arrays)


def pack_by_copies(arrays, zs, places, width):
    rows, features = arrays[0].shape
    count, group = len(arrays), features // zs

    def body(*refs):
        out, sem = refs[count], refs[count + 1]
        copies = []
        for z in range(zs):
            for p, low in enumerate(places):
                for n in range(count):
                    source = refs[n].at[:, pl.ds(z * group + low, width)]
                    target = out.at[p, z, :, pl.ds(n * width, width)]
                    copies.append(pltpu.make_async_copy(source, target, sem.at[len(copies)]))
                    copies[-1].start()
        for copy in copies:
            copy.wait()

    return pl.pallas_call(
        body,
        in_specs=[pl.BlockSpec(memory_space=pl.ANY)] * count,
        out_specs=pl.BlockSpec(memory_space=pltpu.VMEM),
        out_shape=jax.ShapeDtypeStruct((len(places), zs, rows, count * width), arrays[0].dtype),
        scratch_shapes=[pltpu.SemaphoreType.DMA((zs * len(places) * count,))],
        compiler_params=pltpu.CompilerParams(vmem_limit_bytes=58 * 2**20),
        cost_estimate=moved_bytes(4 * count * rows * zs * len(places) * width),
        name="pack_by_copies",
    )(*arrays)


def unpack_tokens(moved, places, width, features, count):
    _, zs, rows, _ = moved.shape
    group = features // zs

    def body(moved_ref, *outs):
        for p, low in enumerate(places):
            for n in range(count):
                outs[n][:, low : low + width] = moved_ref[p, 0, :, n * width : (n + 1) * width]

    return pl.pallas_call(
        body,
        grid=(zs,),
        in_specs=[pl.BlockSpec((moved.shape[0], 1, rows, moved.shape[3]), lambda z: (0, z, 0, 0))],
        out_specs=[pl.BlockSpec((rows, group), lambda z: (0, z))] * count,
        out_shape=[jax.ShapeDtypeStruct((rows, features), moved.dtype)] * count,
        cost_estimate=moved_bytes(4 * count * rows * features),
        name="unpack_tokens",
    )(moved)


def add_tokens(moved, places, width, into):
    _, zs, rows, _ = moved.shape
    count = len(into)
    group = into[0].shape[1] // zs

    def body(moved_ref, *refs):
        outs, sem = refs[count : 2 * count], refs[-1]
        copies = []
        for z in range(zs):
            for p, low in enumerate(places):
                for n in range(count):
                    source = moved_ref.at[p, z, :, pl.ds(n * width, width)]
                    target = outs[n].at[:, pl.ds(z * group + low, width)]
                    copies.append(pltpu.make_async_copy(source, target, sem.at[len(copies)]))
                    copies[-1].start()
        for copy in copies:
            copy.wait()

    anywhere = pl.BlockSpec(memory_space=pl.ANY)
    return pl.pallas_call(
        body,
        in_specs=[pl.BlockSpec(memory_space=pltpu.VMEM)] + [anywhere] * count,
        out_specs=[anywhere] * count,
        out_shape=[jax.ShapeDtypeStruct(a.shape, a.dtype) for a in into],
        scratch_shapes=[pltpu.SemaphoreType.DMA((zs * len(places) * count,))],
        input_output_aliases={n + 1: n for n in range(count)},
        cost_estimate=moved_bytes(4 * count * rows * zs * len(places) * width),
        name="add_tokens",
    )(moved, *into)


def pack_cache(cache_k, cache_v, order, cuts):
    rows, features = cache_k.shape
    parts = order.shape[0]
    group = features // parts

    def body(order_ref, k_ref, v_ref, *outs):
        for p in range(parts):

            @pl.when(pl.program_id(0) == p)
            def _(p=p):
                for s, (low, high) in enumerate(cuts):
                    outs[s * parts + p][:, : high - low] = k_ref[:, low:high]
                    outs[s * parts + p][:, high - low :] = v_ref[:, low:high]

    widths = [2 * (high - low) for low, high in cuts for _ in range(parts)]
    outs = pl.pallas_call(
        body,
        grid_spec=pltpu.PrefetchScalarGridSpec(
            num_scalar_prefetch=1,
            grid=(parts,),
            in_specs=[pl.BlockSpec((rows, group), lambda p, order: (0, order[p]))] * 2,
            out_specs=[pl.BlockSpec((rows, w), lambda p, order: (0, 0)) for w in widths],
        ),
        out_shape=[jax.ShapeDtypeStruct((rows, w), cache_k.dtype) for w in widths],
        compiler_params=pltpu.CompilerParams(vmem_limit_bytes=32 * 2**20),
        cost_estimate=moved_bytes(8 * rows * features),
        name="pack_cache",
    )(order, cache_k, cache_v)
    return [outs[s * parts : (s + 1) * parts] for s in range(len(cuts))]


def sum_cores(mine_k, mine_v, recv_k, recv_v, parts):
    rows, width = mine_k.shape[0] // parts, mine_k.shape[1]

    def body(mine_k_ref, mine_v_ref, recv_k_ref, recv_v_ref, *outs):
        for p in range(parts):

            @pl.when(pl.program_id(0) == p)
            def _(p=p):
                outs[p][:, :width] = (mine_k_ref[...] + recv_k_ref[...]).astype(outs[p].dtype)
                outs[p][:, width:] = (mine_v_ref[...] + recv_v_ref[...]).astype(outs[p].dtype)

    return pl.pallas_call(
        body,
        grid=(parts,),
        in_specs=[pl.BlockSpec((rows, width), lambda p: (p, 0))] * 4,
        out_specs=[pl.BlockSpec((rows, 2 * width), lambda p: (0, 0))] * parts,
        out_shape=[jax.ShapeDtypeStruct((rows, 2 * width), jnp.bfloat16)] * parts,
        compiler_params=pltpu.CompilerParams(vmem_limit_bytes=32 * 2**20),
        cost_estimate=moved_bytes(20 * parts * rows * width),
        name="sum_cores",
    )(mine_k, mine_v, recv_k, recv_v)


def merge_cores(first, mine_k, mine_v, recv_k, recv_v, parts):
    rows, width = mine_k.shape[0] // parts, mine_k.shape[1]

    def body(first_ref, mine_k_ref, mine_v_ref, recv_k_ref, recv_v_ref, *outs):
        mine = pl.multiple_of(first_ref[0] * width, width)
        recv = pl.multiple_of((1 - first_ref[0]) * width, width)
        for p in range(parts):

            @pl.when(pl.program_id(0) == p)
            def _(p=p):
                outs[p][:, pl.ds(mine, width)] = mine_k_ref[...]
                outs[p][:, pl.ds(recv, width)] = recv_k_ref[...]
                outs[p][:, pl.ds(mine + 2 * width, width)] = mine_v_ref[...]
                outs[p][:, pl.ds(recv + 2 * width, width)] = recv_v_ref[...]

    return pl.pallas_call(
        body,
        grid_spec=pltpu.PrefetchScalarGridSpec(
            num_scalar_prefetch=1,
            grid=(parts,),
            in_specs=[pl.BlockSpec((rows, width), lambda p, first: (p, 0))] * 4,
            out_specs=[pl.BlockSpec((rows, 4 * width), lambda p, first: (0, 0))] * parts,
        ),
        out_shape=[jax.ShapeDtypeStruct((rows, 4 * width), jnp.bfloat16)] * parts,
        compiler_params=pltpu.CompilerParams(vmem_limit_bytes=32 * 2**20),
        cost_estimate=moved_bytes(16 * parts * rows * width),
        name="merge_cores",
    )(first, mine_k, mine_v, recv_k, recv_v)


def place_cache(stages, order, cuts):
    parts = order.shape[0]
    rows, group = stages[0][0].shape[0], cuts[-1][1]
    arrays = [a for stage in stages for a in stage]

    def body(order_ref, *refs):
        k_ref, v_ref = refs[len(arrays) :]
        for p in range(parts):

            @pl.when(pl.program_id(0) == p)
            def _(p=p):
                for s, (low, high) in enumerate(cuts):
                    k_ref[:, low:high] = refs[s * parts + p][:, : high - low]
                    v_ref[:, low:high] = refs[s * parts + p][:, high - low :]

    return pl.pallas_call(
        body,
        grid_spec=pltpu.PrefetchScalarGridSpec(
            num_scalar_prefetch=1,
            grid=(parts,),
            in_specs=[pl.BlockSpec(a.shape, lambda p, order: (0, 0)) for a in arrays],
            out_specs=[pl.BlockSpec((rows, group), lambda p, order: (0, order[p]))] * 2,
        ),
        out_shape=[jax.ShapeDtypeStruct((rows, parts * group), arrays[0].dtype)] * 2,
        compiler_params=pltpu.CompilerParams(vmem_limit_bytes=32 * 2**20),
        cost_estimate=moved_bytes(8 * rows * parts * group),
        name="place_cache",
    )(order, *arrays)


def finish_tokens(back_at, back_on, dq, dk, dv, back_k, back_v):
    tokens, width = dq.shape

    def body(back_at_ref, back_on_ref, dq_ref, dk_ref, dv_ref, back_k_ref, back_v_ref, out_ref):
        on = back_on_ref[pl.program_id(0)] > 0
        out_ref[:, :width] = dq_ref[...]
        out_ref[:, width : 2 * width] = (dk_ref[...] + jnp.where(on, back_k_ref[...].astype(jnp.float32), 0.0)).astype(out_ref.dtype)
        out_ref[:, 2 * width :] = (dv_ref[...] + jnp.where(on, back_v_ref[...].astype(jnp.float32), 0.0)).astype(out_ref.dtype)

    own = pl.BlockSpec((WINDOW, width), lambda j, at, on: (j, 0))
    back = pl.BlockSpec((WINDOW, width), lambda j, at, on: (at[j], 0))
    return pl.pallas_call(
        body,
        grid_spec=pltpu.PrefetchScalarGridSpec(
            num_scalar_prefetch=2,
            grid=(tokens // WINDOW,),
            in_specs=[own, own, own, back, back],
            out_specs=pl.BlockSpec((WINDOW, 3 * width), lambda j, at, on: (j, 0)),
        ),
        out_shape=jax.ShapeDtypeStruct((tokens, 3 * width), jnp.bfloat16),
        compiler_params=pltpu.CompilerParams(vmem_limit_bytes=32 * 2**20),
        cost_estimate=moved_bytes(24 * tokens * width),
        name="finish_tokens",
    )(back_at, back_on, dq, dk, dv, back_k, back_v)


def attention_kernel(parts, outs, linked, slots_ref, reads_ref, before_ref, start_ref, order_ref, first_ref, *refs):
    q_ref, do_ref, k_ref, v_ref = refs[:4]
    refs = refs[4:]
    if not linked:
        kt_ref, vt_ref = refs[:2]
        refs = refs[2:]
    ck_refs, cv_refs, refs = refs[:parts], refs[parts : 2 * parts], refs[2 * parts :]
    if linked:
        grads_ref = refs[0]
        refs = refs[1:]
    else:
        dq_ref, dk_ref, dv_ref, dkt_ref, dvt_ref = refs[:5]
        refs = refs[5:]
    gk_refs, gv_refs, refs = refs[:outs], refs[outs : 2 * outs], refs[2 * outs :]
    kx, vx, dkx, dvx = refs[:4]
    if parts > 1:
        ckx, cvx, gkx, gvx = refs[4:]
    else:
        ckx, cvx, gkx, gvx = ck_refs[0], cv_refs[0], gk_refs[0], gv_refs[0]
    rows = q_ref.shape[0]
    span = WINDOW + TILE
    chunk, chunks = pl.program_id(1), pl.num_programs(1)
    group = (first_ref[0] + pl.program_id(0)) // GROUP_HEADS
    table = (group * chunks + order_ref[chunk]) * (rows // BLOCK)

    if linked:
        for ref in (kx, vx, dkx, dvx):
            ref[:WINDOW] = ref[WINDOW:]

        @pl.when(chunk == 0)
        def _():
            for ref in (kx, vx, dkx, dvx):
                ref[:WINDOW] = jnp.zeros((WINDOW, HEAD_DIM), ref.dtype)

        dkx[WINDOW:] = jnp.zeros((WINDOW, HEAD_DIM), jnp.float32)
        dvx[WINDOW:] = jnp.zeros((WINDOW, HEAD_DIM), jnp.float32)
    else:
        kx[:WINDOW] = kt_ref[...]
        vx[:WINDOW] = vt_ref[...]
        dkx[...] = jnp.zeros_like(dkx)
        dvx[...] = jnp.zeros_like(dvx)
    kx[WINDOW:] = k_ref[...]
    vx[WINDOW:] = v_ref[...]

    @pl.when(chunk == 0)
    def _():
        gkx[...] = jnp.zeros_like(gkx)
        gvx[...] = jnp.zeros_like(gvx)
        if parts > 1:
            part_rows = ck_refs[0].shape[0]
            for p in range(parts):
                ckx[p * part_rows : (p + 1) * part_rows] = ck_refs[p][...]
                cvx[p * part_rows : (p + 1) * part_rows] = cv_refs[p][...]

    key_at = lax.broadcasted_iota(jnp.int32, (TILE, TILE), 0)
    query_at = lax.broadcasted_iota(jnp.int32, (TILE, TILE), 1)
    first_half = lax.broadcasted_iota(jnp.int32, (1, TILE), 1) < BLOCK
    first_rows = lax.broadcasted_iota(jnp.int32, (TILE, 1), 0) < BLOCK
    at_start = start_ref[chunk]

    def tile(t, carry):
        at = pl.multiple_of(t * TILE, TILE)
        q = q_ref[pl.ds(at, TILE)]
        do = do_ref[pl.ds(at, TILE)]
        k_loc = kx[pl.ds(at, span)]
        v_loc = vx[pl.ds(at, span)]
        places = []
        k_mem, v_mem = [], []
        for b in range(TILE // BLOCK):
            block = (table + t * (TILE // BLOCK) + b) * READS
            where = [pl.multiple_of(slots_ref[reads_ref[block + r]] * BLOCK, BLOCK) for r in range(READS)]
            places.append(where)
            k_mem.append(jnp.concatenate([ckx[pl.ds(w, BLOCK)] for w in where], 0))
            v_mem.append(jnp.concatenate([cvx[pl.ds(w, BLOCK)] for w in where], 0))

        s_loc = dot(k_loc, q, (1, 1))
        s_mem = jnp.where(first_half, dot(k_mem[0], q, (1, 1)), dot(k_mem[1], q, (1, 1)))
        pieces = []
        for c in range(span // TILE):
            piece = s_loc[c * TILE : (c + 1) * TILE]
            if c < span // TILE - 1:
                before = (at_start > 0) & (at + c * TILE < WINDOW)
                piece = piece + jnp.where(before, MASKED, 0.0)
            else:
                piece = jnp.where(key_at <= query_at, piece, MASKED)
            if c == 0:
                piece = jnp.where(key_at >= query_at, piece, MASKED)
            pieces.append(piece)
        s_loc = jnp.concatenate(pieces, 0)
        top = jnp.maximum(jnp.max(s_loc, 0, keepdims=True), jnp.max(s_mem, 0, keepdims=True))
        unit = SCALE * math.log2(math.e)
        e_loc = jnp.exp2((s_loc - top) * unit)
        e_mem = jnp.exp2((s_mem - top) * unit)
        total = jnp.sum(e_loc, 0, keepdims=True) + jnp.sum(e_mem, 0, keepdims=True)
        inverse = 1.0 / total
        p_loc = e_loc * inverse
        p_mem = e_mem * inverse
        w_loc = p_loc.astype(jnp.bfloat16)
        w_mem = p_mem.astype(jnp.bfloat16)
        dp_loc = dot(v_loc, do, (1, 1))
        dp_mem = jnp.where(first_half, dot(v_mem[0], do, (1, 1)), dot(v_mem[1], do, (1, 1)))
        delta = jnp.sum(w_loc.astype(jnp.float32) * dp_loc, 0, keepdims=True) + jnp.sum(
            w_mem.astype(jnp.float32) * dp_mem, 0, keepdims=True
        )
        ds_loc = (p_loc * (dp_loc - delta)).astype(jnp.bfloat16)
        ds_mem = (p_mem * (dp_mem - delta)).astype(jnp.bfloat16)

        dq_mem = jnp.where(first_rows, dot(ds_mem, k_mem[0], (0, 0)), dot(ds_mem, k_mem[1], (0, 0)))
        dq = ((dot(ds_loc, k_loc, (0, 0)) + dq_mem) * SCALE).astype(jnp.bfloat16)
        if linked:
            grads_ref[pl.ds(pl.multiple_of(chunk * rows + at, TILE), TILE), :HEAD_DIM] = dq
        else:
            dq_ref[pl.ds(at, TILE)] = dq
        dkx[pl.ds(at, span)] += dot(ds_loc, q, (1, 0))
        dvx[pl.ds(at, span)] += dot(w_loc, do, (1, 0))
        zero = jnp.zeros_like(q)
        q_two = jnp.concatenate([jnp.where(first_rows, q, zero), jnp.where(first_rows, zero, q)], 1)
        do_two = jnp.concatenate([jnp.where(first_rows, do, zero), jnp.where(first_rows, zero, do)], 1)
        read_k = (dot(ds_mem, q_two, (1, 0)) * SCALE).astype(jnp.bfloat16).astype(jnp.float32)
        read_v = dot(w_mem, do_two, (1, 0)).astype(jnp.bfloat16).astype(jnp.float32)
        for b in range(TILE // BLOCK):
            for r in range(READS):
                here = (slice(r * BLOCK, (r + 1) * BLOCK), slice(b * HEAD_DIM, (b + 1) * HEAD_DIM))
                gkx[pl.ds(places[b][r], BLOCK)] += read_k[here]
                gvx[pl.ds(places[b][r], BLOCK)] += read_v[here]
        return carry

    lax.fori_loop(0, rows // TILE, tile, 0, unroll=UNROLL)
    if linked:

        def put(first, low):
            there = pl.ds(pl.multiple_of(first, WINDOW), WINDOW)
            here = slice(low, low + WINDOW)
            grads_ref[there, HEAD_DIM : 2 * HEAD_DIM] = (dkx[here] * SCALE).astype(grads_ref.dtype)
            grads_ref[there, 2 * HEAD_DIM :] = dvx[here].astype(grads_ref.dtype)

        @pl.when(chunk > 0)
        def _():
            put((chunk - 1) * WINDOW, 0)

        @pl.when(chunk == chunks - 1)
        def _():
            put(chunk * WINDOW, WINDOW)

    else:
        dkt_ref[...] = (dkx[:WINDOW] * SCALE).astype(dkt_ref.dtype)
        dvt_ref[...] = dvx[:WINDOW].astype(dvt_ref.dtype)
        dk_ref[...] = dkx[WINDOW:] * SCALE
        dv_ref[...] = dvx[WINDOW:]
    if parts > 1:

        @pl.when(chunk == chunks - 1)
        def _():
            out_rows = gk_refs[0].shape[0]
            for p in range(outs):
                gk_refs[p][...] = gkx[p * out_rows : (p + 1) * out_rows].astype(gk_refs[p].dtype)
                gv_refs[p][...] = gvx[p * out_rows : (p + 1) * out_rows].astype(gv_refs[p].dtype)


def attention(tables, tokens_in, prev, cache):
    rows, width = tokens_in.shape[0], tokens_in.shape[1] // 4
    heads = width // HEAD_DIM
    cache_heads = cache[0].shape[1] // (2 * HEAD_DIM)
    parts, part_rows = len(cache), cache[0].shape[0]
    outs = min(2, parts)
    out_rows = parts * part_rows // outs
    linked = prev is None

    def chunk_of(offset):
        return pl.BlockSpec((WINDOW, HEAD_DIM), lambda h, j, *_: (j, h + offset))

    def before(offset):
        return pl.BlockSpec((WINDOW, HEAD_DIM), lambda h, j, slots, reads, at, *_: (at[j], h + offset))

    def column(height):
        return pl.BlockSpec((height, HEAD_DIM), lambda h, j, *_: (0, h))

    def cached(offset):
        return pl.BlockSpec((part_rows, HEAD_DIM), lambda h, j, *tables: (0, h + tables[-1][0] + offset))

    bf16, f32 = jnp.bfloat16, jnp.float32
    shape = jax.ShapeDtypeStruct
    scratch = [pltpu.VMEM((2 * WINDOW, HEAD_DIM), kind) for kind in (bf16, bf16, f32, f32)]
    if parts > 1:
        scratch += [pltpu.VMEM((parts * part_rows, HEAD_DIM), kind) for kind in (bf16, bf16, f32, f32)]
    if linked:
        token_specs = [pl.BlockSpec((rows, 3 * HEAD_DIM), lambda h, j, *_: (0, h))]
        token_shapes = [shape((rows, 3 * width), bf16)]
    else:
        token_specs = [chunk_of(0)] * 5
        token_shapes = [shape((rows, width), kind) for kind in (bf16, f32, f32, bf16, bf16)]
    pairs = heads * rows * (WINDOW + TILE + 2 * READS * BLOCK)
    results = pl.pallas_call(
        functools.partial(attention_kernel, parts, outs, linked),
        grid_spec=pltpu.PrefetchScalarGridSpec(
            num_scalar_prefetch=6,
            grid=(heads, rows // WINDOW),
            in_specs=[chunk_of(n * heads) for n in range(4)]
            + ([] if linked else [before(0), before(heads)])
            + [cached(0)] * parts
            + [cached(cache_heads)] * parts,
            out_specs=token_specs + [column(out_rows)] * (2 * outs),
            scratch_shapes=scratch,
        ),
        out_shape=token_shapes + [shape((out_rows, width), bf16 if linked else f32)] * (2 * outs),
        compiler_params=pltpu.CompilerParams(vmem_limit_bytes=56 * 2**20),
        cost_estimate=pl.CostEstimate(
            flops=10 * pairs * HEAD_DIM, bytes_accessed=heads * part_rows * parts * 3000, transcendentals=pairs
        ),
        name="attention",
    )(*tables, *[tokens_in] * 4, *([] if linked else [prev, prev]), *cache, *cache)
    count = len(token_specs)
    return results[:count], results[count : count + outs], results[count + outs :]


def per_device(queries, keys_local, values_local, cache_keys, cache_values, block_map, retrieved, out_grad):
    chips, zs = lax.axis_size("chip"), lax.axis_size("head")
    chip, core = lax.axis_index("chip"), lax.axis_index("core")
    rows, features = queries.shape
    cache_rows = cache_keys.shape[0]
    blk_dev = cache_rows // BLOCK
    groups = retrieved.shape[1]
    shared = groups == chips and chips in (2, 4)
    split = chips if shared else 1
    group_width = features // (split * zs)
    low = 2 * HEAD_DIM
    cuts = ((0, low), (low, group_width))
    firsts = [g * group_width for g in range(split)]
    if shared:
        axes = (("chip", "core", "head"), ("chip", "head"))
        plan = (([g + c * HEAD_DIM for g in firsts for c in range(2)], HEAD_DIM), ([g + low for g in firsts], HEAD_DIM))
    else:
        axes = (("head",), ("head",))
        plan = tuple(([g + a for g in firsts], b - a) for a, b in cuts)
    seq_parts = min(8, 2 * chips)
    bf16 = jnp.bfloat16

    def exchange(array, stage):
        return lax.all_to_all(array, axes[stage], split_axis=0, concat_axis=0, tiled=True)

    def to_heads(packed, stage):
        places, _, _, width = packed.shape
        return exchange(packed.reshape(places * zs, rows, width), stage).reshape(places * zs * rows, width)

    def to_tokens(array, stage):
        places, width = len(plan[stage][0]), array.shape[1]
        return exchange(array.reshape(places * zs, rows, width), stage).reshape(places, zs, rows, width)

    def other_core(array):
        return lax.ppermute(array, "core", [(0, 1), (1, 0)])

    def other_chip(array, by):
        return lax.ppermute(array, "chip", [(i, i ^ by) for i in range(chips)]) if by else array

    def ints(*arrays):
        return tuple(a.astype(jnp.int32) for a in arrays)

    everyone = ("chip", "core")
    parts = 2 * chips
    owner, local = block_map // blk_dev, block_map % blk_dev
    if shared:
        chip_order = jnp.arange(chips, dtype=jnp.int32) ^ chip
        arrived = [other_chip(retrieved, k) for k in range(chips)]
        ids = lax.dynamic_slice_in_dim(jnp.stack(arrived), chip, 1, 2)
        reads = jnp.concatenate([ids.reshape(-1), other_core(ids).reshape(-1)])
        slots = (((owner % 2) ^ core) * chips + ((owner // 2) ^ chip)) * blk_dev + local
        mem = jnp.arange(parts, dtype=jnp.int32)
        start_a = (mem % seq_parts == 0) + 0 * mem
        order_a = ((mem % 2) ^ core) * chips + ((mem // 2) ^ chip)
        tables_a = ints(slots, reads, mem, start_a, order_a, core.reshape(1))
        numbers = jnp.arange(chips, dtype=jnp.int32)
        before, back_at = jnp.maximum(numbers - 1 + core, 0), jnp.minimum(numbers + core, chips - 1)
        back_on = numbers + core < chips
        start_b = (2 * numbers + core) % seq_parts == 0
        tables_b = ints(slots, reads, before, start_b, chip_order, jnp.zeros((1,)))
        backs = ints(back_at, back_on)
    else:
        zero = jnp.zeros((1,), jnp.int32)
        reads = jnp.transpose(retrieved, (1, 0, 2)).reshape(-1)
        start = (lax.axis_index(everyone) % seq_parts == 0).reshape(1)
        tables_a = ints(block_map, reads, zero, start, zero, zero)
        tables_b = ints(block_map, reads, zero, start, zero, zero + low // HEAD_DIM)
        backs = (zero, zero + 1)
    tables = (tables_a, tables_b)

    token_arrays = [queries, out_grad, keys_local, values_local]
    packed_b = pack_by_copies(token_arrays, zs, *plan[1])
    (packed_a,) = pack_tokens(token_arrays, zs, plan[:1])
    if shared:
        pieces = pack_cache(cache_keys, cache_values, chip_order, cuts)
    else:
        cache_a = cache_b = [lax.all_gather(jnp.concatenate([cache_keys, cache_values], 1), everyone, tiled=True)]

    def spread(pieces):
        mine = [other_chip(piece, k) for k, piece in enumerate(pieces)]
        return mine + [other_core(piece) for piece in mine], mine

    def chunks_before(keys_values):
        if shared:
            return other_core(keys_values)
        return lax.ppermute(keys_values, everyone, [(i, i + 1) for i in range(parts - 1)])

    def send_back(grads):
        if shared:
            return other_core(grads)
        return lax.ppermute(grads, everyone, [(i + 1, i) for i in range(parts - 1)])

    def by_tokens(stage, moved, cache):
        width = moved.shape[1] // 4
        prev = chunks_before(moved[:, 2 * width :])
        (dq, dk, dv, dkt, dvt), gk, gv = attention(tables[stage], moved, prev, cache)
        out = finish_tokens(*backs, dq, dk, dv, send_back(dkt), send_back(dvt))
        if not shared:
            return out, [lax.psum_scatter(g[0], everyone, scatter_dimension=0, tiled=True).astype(bf16) for g in (gk, gv)]
        return out, sum_cores(gk[0], gv[0], other_core(gk[1]), other_core(gv[1]), chips)

    def by_heads(stage, moved, cache):
        (out,), gk, gv = attention(tables[stage], moved, None, cache)
        return out, (gk, gv)

    moved_b = to_heads(packed_b, 1)
    early = ()
    if shared:
        cache_b, mine = spread(pieces[1])
        early = (mine, arrived)
    moved_b, packed_a, early = after((moved_b, packed_a, early), ())
    if shared:
        cache_a, _ = spread(after(pieces[0], moved_b))
    moved_a = to_heads(packed_a, 0)
    out_b, sums_b = by_tokens(1, moved_b, cache_b)
    moved_a, out_b, sums_b, tables, cache_a = after((moved_a, out_b, sums_b, tables, cache_a), ())
    out_b = to_tokens(out_b, 1)
    out_a, sums_a = (by_heads if shared else by_tokens)(0, moved_a, cache_a)
    if shared:
        sums_b = [other_chip(s, k) for k, s in enumerate(sums_b)]
    out_a, out_b, sums_b = after((out_a, out_b, sums_b), ())
    if shared:
        gk, gv = sums_a
        sums_a = merge_cores(tables_a[5], gk[0], gv[0], other_core(gk[1]), other_core(gv[1]), chips)
        sums_a = [other_chip(s, k) for k, s in enumerate(sums_a)]
        grad_cache = place_cache([sums_a, sums_b], chip_order, cuts)
    else:
        grad_cache = [jnp.concatenate([a, b], 1) for a, b in zip(sums_a, sums_b)]
    grads = unpack_tokens(out_b, *plan[1], features, 3)
    out_a = to_tokens(out_a, 0)
    return (*add_tokens(out_a, *plan[0], grads), *grad_cache)


def solution(mesh):
    shape = mesh.shape
    fine = Mesh(mesh.devices.reshape(shape["mem"] // 2, 2, shape["head"]), ("chip", "core", "head"))
    by_token = P(("chip", "core", "head"), None)
    by_block = P(("chip", "core"), "head")
    return jax.shard_map(
        per_device,
        mesh=fine,
        in_specs=(
            by_token,
            by_token,
            by_token,
            by_block,
            by_block,
            P(),
            P(("chip", "core"), "head", None),
            by_token,
        ),
        out_specs=(by_token, by_token, by_token, by_block, by_block),
        check_vma=False,
    )
```
